512 devices in a mesh: dp: 16 (over y_hi, x), tp: 32 (over z, y_lo, core).
Axes of the slice: x: 4, y: 8 (y_hi: 4, y_lo: 2; y = y_hi * 2 + y_lo), z: 8, core: 2. Of those that a mesh axis runs over, the one named last changes fastest.
Arguments:
- queries: bfloat16 [16, 32, 2, 8192], P('dp', 'tp'), may hold values from -124 to 124
- residual: bfloat16 [16, 32, 2, 8192], P('dp', 'tp'), may hold values from -40 to 40
- new_entries: bfloat16 [16, 32, 2, 2048], P('dp', 'tp'), may hold values from -6 to 6
- page_pool: bfloat16 [16, 32, 32, 16, 2048], P('dp', 'tp'), may hold values from -5.6 to 5.6
- page_table: int32 [16, 32, 2, 16], P('dp', 'tp'), may hold values from 0 to 31, as said below
- cache_lengths: int32 [16, 32, 2], P('dp', 'tp'), may hold values from 1 to 256
- migration: int32 [32, 3, 3], P('tp'), may hold values from 0 to 15, as said below
- norm_gain: bfloat16 [8192], replicated, may hold values from 0.5 to 1.5
- gate_weight: bfloat16 [8192, 16384], P('dp', 'tp'), may hold values from -0.0625 to 0.0625
- up_weight: bfloat16 [8192, 16384], P('dp', 'tp'), may hold values from -0.0625 to 0.0625
- down_weight: bfloat16 [16384, 8192], P('tp', 'dp'), may hold values from -0.046875 to 0.046875
Outputs:
- layer_out: bfloat16 [16, 32, 2, 8192], P('dp', 'tp')
The draws below stay inside these ranges and needn't reach their ends.
Inputs may be any that keep to these rules, and one draw needn't show every extreme that they name: `page_table`: each device's page tables name each of its 32 pool pages once. `migration`: for each tp index the 3 entries name one slot and 3 distinct source ranks; each entry's destination is the next entry's source, the last entry's destination the first entry's source.
All inputs are finite; a program needn't handle non-finite values.
Results may differ from the reference program's by a relative error of at most 0.014.
Values may be sent and summed in bfloat16 or wider, within the bound.
A program may use at most 64 MiB of HBM per device.

```python
import math
import jax
import jax.numpy as jnp
from jax import lax

D = 8192
HQ = 64
KVH = 8
HD = 128
FF = 16384
S = 2
MAXP = 16
PG = 16
MIG = 3
MAXL = 256
KVW = 2048
N_DP = 16
N_TP = 32


def draw_queries(key, part):
    key = jax.random.fold_in(key, 11)
    noise_key = jax.random.fold_in(key, 0)
    values = jnp.clip(jax.random.normal(noise_key, (N_DP, N_TP, S, KVH, HQ // KVH, HD), jnp.float32), -4.0, 4.0)
    return values.reshape(N_DP, N_TP, S, HQ * HD).astype(jnp.bfloat16)


def draw_page_pool(key, part):
    key = jax.random.fold_in(key, 12)
    key_part, value_part = jax.random.split(key)
    key_values = jnp.clip(jax.random.normal(key_part, (N_DP, N_TP, S * MAXP, PG, KVH, HD), jnp.float32), -4.0, 4.0)
    value_values = jnp.clip(jax.random.normal(value_part, (N_DP, N_TP, S * MAXP, PG, KVH, HD), jnp.float32), -4.0, 4.0)
    joined = jnp.concatenate([key_values.reshape(N_DP, N_TP, S * MAXP, PG, KVH * HD), value_values.reshape(N_DP, N_TP, S * MAXP, PG, KVH * HD)], axis=-1)
    return joined.astype(jnp.bfloat16)


def draw_residual(key, part):
    key = jax.random.fold_in(key, 13)
    column_key, row_key, base_key = jax.random.split(key, 3)
    row_total = N_DP * N_TP * S
    column_scale = 10.0 ** jax.random.uniform(column_key, (D,), jnp.float32, -0.5, 0.5)
    row_scale = 10.0 ** jax.random.uniform(row_key, (row_total, 1), jnp.float32, -0.5, 0.5)
    base = jnp.clip(jax.random.normal(base_key, (row_total, D), jnp.float32), -4.0, 4.0)
    return (base * column_scale * row_scale).reshape(N_DP, N_TP, S, D).astype(jnp.bfloat16)


def draw_cache_lengths(key, part):
    key = jax.random.fold_in(key, 14)
    limit_key, length_key, pick_key = jax.random.split(key, 3)
    limits = jax.random.randint(limit_key, (N_DP, N_TP, 1), MAXL // 8, MAXL + 1)
    lengths = jnp.minimum(jax.random.randint(length_key, (N_DP, N_TP, S), 1, MAXL + 1), limits)
    chosen = jax.random.randint(pick_key, (), 0, N_DP * N_TP * S)
    flat_lengths = lengths.reshape(-1)
    flat_lengths = jnp.where(jnp.arange(N_DP * N_TP * S) == chosen, MAXL, flat_lengths)
    return flat_lengths.reshape(N_DP, N_TP, S).astype(jnp.int32)


def draw_page_table(key, part):
    key = jax.random.fold_in(key, 15)
    device_keys = jax.random.split(key, N_DP * N_TP)
    orders = jax.vmap(lambda device_key: jax.random.permutation(device_key, S * MAXP))(device_keys)
    return orders.reshape(N_DP, N_TP, S, MAXP).astype(jnp.int32)


def draw_migration(key, part):
    key = jax.random.fold_in(key, 16)
    rank_key, slot_key = jax.random.split(key)
    column_keys = jax.random.split(rank_key, N_TP)
    sources = jax.vmap(lambda column_key: jax.random.permutation(column_key, N_DP)[:MIG])(column_keys)
    targets = jnp.roll(sources, -1, axis=1)
    slot_ids = jnp.broadcast_to(jax.random.randint(slot_key, (N_TP, 1), 0, S), (N_TP, MIG))
    return jnp.stack([slot_ids, sources, targets], axis=-1).astype(jnp.int32)


def levels(key, dims, pieces, low, top_value):
    level, own = 1.0, jax.random.fold_in(key, 6)
    for axis_at, shards_of in pieces:
        heights = jnp.exp(jax.random.uniform(jax.random.fold_in(own, axis_at), (shards_of,), jnp.float32, low / len(pieces), top_value / len(pieces)))
        level = level * jnp.repeat(heights, dims[axis_at] // shards_of).reshape([-1 if axis == axis_at else 1 for axis in range(len(dims))])
    return level


def noise(rng, extent, deviation, limit, pieces=(), kind=jnp.bfloat16):
    factor_of = levels(rng, extent, pieces, -0.22, 0.18) if pieces else 1.0
    entries = jax.random.normal(rng, extent, jnp.float32) * deviation * factor_of
    return jnp.minimum(jnp.maximum(entries, -limit), limit).astype(kind)


def setup_inputs(seed: int = 0) -> dict:
    arg_keys = jax.random.split(jax.random.key(seed), 12)
    queries = draw_queries(jax.random.fold_in(arg_keys[11], 71), 0)
    residual = draw_residual(jax.random.fold_in(arg_keys[11], 71), 0)
    new_entries = noise(arg_keys[2], (N_DP, N_TP, S, KVW), 1.0, 6.0, ((0, 16), (1, 32)))
    page_pool = draw_page_pool(jax.random.fold_in(arg_keys[11], 71), 0)
    page_table = draw_page_table(jax.random.fold_in(arg_keys[11], 71), 0)
    cache_lengths = draw_cache_lengths(jax.random.fold_in(arg_keys[11], 71), 0)
    migration = draw_migration(jax.random.fold_in(arg_keys[11], 71), 0)
    norm_gain = jnp.clip(1.0 + 0.1 * jax.random.normal(arg_keys[7], (D,), jnp.float32), 0.5, 1.5).astype(jnp.bfloat16)
    gate_weight = noise(arg_keys[8], (D, FF), D ** -0.5, 0.0625, ((0, 16), (1, 32)))
    up_weight = noise(arg_keys[9], (D, FF), D ** -0.5, 0.0625, ((0, 16), (1, 32)))
    down_weight = noise(arg_keys[10], (FF, D), FF ** -0.5, 0.046875, ((0, 32), (1, 16)))
    return {"queries": queries, "residual": residual, "new_entries": new_entries, "page_pool": page_pool, "page_table": page_table, "cache_lengths": cache_lengths, "migration": migration, "norm_gain": norm_gain, "gate_weight": gate_weight, "up_weight": up_weight, "down_weight": down_weight}


epsilon = 1e-05

def settle(values):
    return lax.optimization_barrier(values.astype(jnp.bfloat16)).astype(jnp.float32)

def attend_one(query_row, fresh_row, cache_rows, length):
    groups = HQ // KVH
    factor = 1.0 / math.sqrt(HD)
    head_query = query_row.astype(jnp.float32).reshape(KVH, groups, HD)
    key_rows = cache_rows[:, :KVH * HD].astype(jnp.float32).reshape(MAXL, KVH, HD)
    value_rows = cache_rows[:, KVH * HD:].astype(jnp.float32).reshape(MAXL, KVH, HD)
    own_key = fresh_row[:KVH * HD].astype(jnp.float32).reshape(KVH, HD)
    own_value = fresh_row[KVH * HD:].astype(jnp.float32).reshape(KVH, HD)
    scores = jnp.einsum('kgd,lkd->kgl', head_query, key_rows) * factor
    visible = jnp.arange(MAXL) < length
    scores = jnp.where(visible[None, None, :], scores, -jnp.inf)
    own_score = jnp.einsum('kgd,kd->kg', head_query, own_key) * factor
    highest = jnp.maximum(lax.optimization_barrier(jnp.max(scores, axis=-1)), own_score)
    exponent = jnp.exp(scores - highest[..., None])
    own_exponent = jnp.exp(own_score - highest)
    denominator = lax.optimization_barrier(jnp.sum(exponent, axis=-1)) + own_exponent
    weights = settle(exponent / denominator[..., None])
    own_weight = settle(own_exponent / denominator)
    attended_row = jnp.einsum('kgl,lkd->kgd', weights, value_rows)
    attended_row = attended_row + own_weight[..., None] * own_value[:, None, :]
    return attended_row.reshape(HQ * HD)

def reference(queries, residual, new_entries, page_pool, page_table, cache_lengths, migration, norm_gain, gate_weight, up_weight, down_weight):
    dp_count, tp_count, slot_count = (queries.shape[0], queries.shape[1], queries.shape[2])
    dp_place = jnp.broadcast_to(jnp.arange(dp_count, dtype=jnp.int32)[:, None, None], (dp_count, tp_count, slot_count))
    tp_place = jnp.broadcast_to(jnp.arange(tp_count, dtype=jnp.int32)[None, :, None], (dp_count, tp_count, slot_count))
    slot_place = jnp.broadcast_to(jnp.arange(slot_count, dtype=jnp.int32)[None, None, :], (dp_count, tp_count, slot_count))
    anchor = dp_place
    for entry_index in range(MIG):
        slot_of = migration[:, entry_index, 0][None, :, None]
        source = migration[:, entry_index, 1][None, :, None]
        target = migration[:, entry_index, 2][None, :, None]
        matches = (dp_place == target) & (slot_place == slot_of)
        anchor = jnp.where(matches, source, anchor)

    def one_row(packed):
        source, column, slot_id, query_row, fresh_row = packed
        page_ids = page_table[source, column, slot_id]
        cache_rows = page_pool[source, column][page_ids].reshape(MAXL, KVW)
        return attend_one(query_row, fresh_row, cache_rows, cache_lengths[source, column, slot_id])
    attended = lax.map(one_row, (anchor.reshape(-1), tp_place.reshape(-1), slot_place.reshape(-1), queries.reshape(-1, HQ * HD), new_entries.reshape(-1, KVW)))
    stream = residual.reshape(-1, D).astype(jnp.float32) + attended
    normed = (stream * lax.rsqrt(lax.optimization_barrier(jnp.mean(stream * stream, axis=-1, keepdims=True)) + epsilon) * norm_gain.astype(jnp.float32)).astype(jnp.bfloat16)
    width_piece = D // dp_count
    row_total = normed.shape[0]
    gate = jnp.zeros((row_total, FF), jnp.float32)
    up_sum = jnp.zeros((row_total, FF), jnp.float32)
    for range_index in range(dp_count):
        lower = range_index * width_piece
        upper = lower + width_piece
        gate = gate + settle(jnp.dot(normed[:, lower:upper], gate_weight[lower:upper], preferred_element_type=jnp.float32))
        up_sum = up_sum + settle(jnp.dot(normed[:, lower:upper], up_weight[lower:upper], preferred_element_type=jnp.float32))
    hidden = (jax.nn.silu(gate) * up_sum).astype(jnp.bfloat16)
    ffn = jnp.dot(hidden, down_weight, preferred_element_type=jnp.float32).astype(jnp.bfloat16)
    layer_out = (stream + ffn.astype(jnp.float32)).astype(jnp.bfloat16)
    return layer_out.reshape(dp_count, tp_count, slot_count, D)
```

```python
import functools
import math

import jax
import jax.numpy as jnp
from jax import lax
from jax.experimental import pallas as pl
from jax.experimental.pallas import tpu as pltpu
from jax.sharding import PartitionSpec as P

HD = 128
KVH = 8
NX, NH, NZ = 4, 4, 8
DP = NX * NH
MIG = 3
CHUNKS = ((0, 1), (-3, 4), (-2, 3), (-1, 2))
EPSILON = 1e-05
BF = jnp.bfloat16
F32 = jnp.float32


def kernel(
    plan, own, bias, gain, pool, gate_w, up_w, down_w, out,
    pool_v, gate_v, up_v, down_v,
    route_a, b_send, route_b, c_send, spread_c, tiles, x_all,
    gate_p, up_p, m1g, m1u, m2g, m2u, s3g, s3u, m3g, m3u,
    h_send, h_recv, hid, part, part_in, z_send, z_recv, l_send, l_recv,
    e_send, e_recv,
    load_sem, a_s, a_r, b_s, b_r, c_s, c_r, e_s, e_r,
    xl_s, xl_r, xz_s, xz_r, xc_s, xc_r,
    xp_s, xp_r, hp_s, hp_r, hg_s, hg_r, xg_s, xg_r,
    oc_s, oc_r, oz_s, oz_r, ol_s, ol_r,
):
    dp, tp = lax.axis_index("dp"), lax.axis_index("tp")
    h, x = lax.div(dp, NX), lax.rem(dp, NX)
    z, low = lax.div(tp, 4), lax.rem(tp, 4)
    l, c = lax.div(low, 2), lax.rem(low, 2)
    other_l, other_c = 1 - l, 1 - c
    xr, xo, xl = lax.rem(x + 1, NX), lax.rem(x + 2, NX), lax.rem(x + 3, NX)

    def at_dp(rank):
        return (rank, tp)

    def at_x(place):
        return (h * NX + place, tp)

    def at_h(place):
        return (place * NX + x, tp)

    def at_tp(zz, ll, cc):
        return (dp, zz * 4 + ll * 2 + cc)

    def z_at(offset):
        return lax.rem(z + (offset + NZ), NZ)

    sent = []

    def send(src, dst, send_sem, recv_sem, device):
        copy = pltpu.make_async_remote_copy(
            src_ref=src, dst_ref=dst, send_sem=send_sem, recv_sem=recv_sem,
            device_id=device, device_id_type=pl.DeviceIdType.MESH,
        )
        copy.start()
        sent.append(copy)

    def arrived(dst, send_sem, recv_sem, device):
        pltpu.make_async_remote_copy(
            src_ref=dst, dst_ref=dst, send_sem=send_sem, recv_sem=recv_sem,
            device_id=device, device_id_type=pl.DeviceIdType.MESH,
        ).wait_recv()

    loads = [
        pltpu.make_async_copy(src, dst, load_sem.at[i])
        for i, (src, dst) in enumerate(
            ((pool, pool_v), (gate_w, gate_v), (up_w, up_v), (down_w, down_v))
        )
    ]
    for copy in loads:
        copy.start()

    others = [lax.rem(dp + o, DP) for o in range(1, DP)]
    barrier = pltpu.get_barrier_semaphore()
    partners = [at_dp(rank) for rank in others]
    partners += [at_tp(z_at(o), l, c) for o in range(1, NZ)]
    partners += [at_tp(z, other_l, c), at_tp(z, l, other_c)]
    for device in partners:
        pl.semaphore_signal(barrier, inc=1, device_id=device, device_id_type=pl.DeviceIdType.MESH)
    pl.semaphore_wait(barrier, len(partners))

    def exchange(src_of, dst, s_sem, r_sem):
        for o, rank in enumerate(others):
            send(src_of(rank), dst.at[dp], s_sem.at[o], r_sem.at[o], at_dp(rank))

    def exchanged(dst, s_sem, r_sem):
        for o in range(DP - 1):
            rank = lax.rem(dp + (DP - 1 - o), DP)
            arrived(dst.at[rank], s_sem.at[o], r_sem.at[o], at_dp(rank))

    exchange(lambda rank: own.at[1, rank], route_a, a_s, a_r)
    route_a[dp] = own[1, dp]
    exchanged(route_a, a_s, a_r)
    picked = [route_a[plan[i]].astype(F32) for i in range(MIG)]
    fresh = picked[0][8:] + pltpu.roll(picked[1][8:], 1, 0) + pltpu.roll(picked[2][8:], 2, 0)
    b_send[...] = jnp.concatenate(
        [picked[0][:8], picked[1][:8], picked[2][:8], fresh], axis=0
    ).astype(BF)
    exchange(lambda rank: b_send, route_b, b_s, b_r)
    route_b[dp] = b_send[...]
    exchanged(route_b, b_s, b_r)

    serves = [plan[MIG + i] == dp for i in range(MIG)]
    local = own[0].astype(F32)
    listed = own[1].astype(F32)
    routed = route_b[...].astype(F32)
    row_q = listed[:, :8]
    row_new = listed[:, 8:9]
    for i in range(MIG):
        row_q = jnp.where(serves[i], routed[:, 8 * i : 8 * i + 8], row_q)
        row_new = jnp.where(serves[i], routed[:, 24 + i : 25 + i], row_new)
    upper = lax.broadcasted_iota(jnp.int32, (DP, 8, HD), 1) < 4
    q_tile = jnp.where(upper, local[:, :8], row_q)
    res_tile = jnp.where(upper, row_q, local[:, :8])
    res_tile = jnp.concatenate([res_tile[:, 4:], res_tile[:, :4]], axis=1)
    new_tile = jnp.where(
        upper,
        jnp.broadcast_to(local[:, 8:9], (DP, 8, HD)),
        jnp.broadcast_to(row_new, (DP, 8, HD)),
    )
    q_rows = q_tile.reshape(KVH, 16, HD)
    new_rows = jnp.concatenate([new_tile, new_tile], axis=1)
    new_keys, new_values = new_rows[:KVH], new_rows[KVH:]
    factor = 1.0 / math.sqrt(HD)
    new_score = jnp.sum(q_rows * new_keys, axis=-1, keepdims=True) * factor
    q_bf = q_rows.astype(BF)
    loads[0].wait()
    hidden_bias = bias[...]
    attended = []
    for head in range(KVH):
        keys = pool_v[:, head * HD : (head + 1) * HD]
        score = (
            lax.dot_general(
                q_bf[head], keys, (((1,), (1,)), ((), ())), preferred_element_type=F32
            )
            * factor
            + hidden_bias
        )
        own_score = new_score[head]
        top = jnp.maximum(jnp.max(score, axis=-1, keepdims=True), own_score)
        exponent = jnp.exp(score - top)
        own_exponent = jnp.exp(own_score - top)
        scale = 1.0 / (jnp.sum(exponent, axis=-1, keepdims=True) + own_exponent)
        weight = (exponent * scale).astype(BF)
        own_weight = (own_exponent * scale).astype(BF).astype(F32)
        values = pool_v[:, (KVH + head) * HD : (KVH + head + 1) * HD]
        attended.append(
            jnp.dot(weight, values, preferred_element_type=F32) + own_weight * new_values[head]
        )
    stream = res_tile + jnp.stack(attended).reshape(DP, 8, HD)
    square = jnp.sum(jnp.sum(stream * stream, axis=0), axis=-1, keepdims=True)
    first = lax.broadcasted_iota(jnp.int32, (8, 1), 0) < 4
    width = DP * 4 * HD
    total_0 = jnp.sum(jnp.where(first, square, 0.0), axis=0, keepdims=True)
    total_1 = jnp.sum(jnp.where(first, 0.0, square), axis=0, keepdims=True)
    mean = jnp.where(first, total_0, total_1) * (1.0 / width)
    normed = stream * lax.rsqrt(mean + EPSILON)[None] * gain[...]
    c_send[...] = jnp.concatenate([normed, stream], axis=1).astype(BF)
    exchange(lambda rank: c_send.at[rank], spread_c, c_s, c_r)
    spread_c[dp] = c_send[dp]
    exchanged(spread_c, c_s, c_r)

    tiles[...] = spread_c[:, :8].astype(F32).reshape(DP * 8, HD)
    x_all[z, c, l] = jnp.concatenate(
        [tiles[pl.ds(i, 32, stride=4), :] for i in range(4)], axis=1
    ).astype(BF)
    send(x_all.at[z, c, l], x_all.at[z, c, l], xl_s, xl_r, at_tp(z, other_l, c))
    arrived(x_all.at[z, c, other_l], xl_s, xl_r, at_tp(z, other_l, c))
    offsets = [o for chunk in CHUNKS for o in chunk]

    def slot(offset):
        return (offset + NZ) % NZ

    send(x_all.at[z, c], x_all.at[z, c], xc_s.at[0], xc_r.at[0], at_tp(z, l, other_c))
    for o in offsets[1:]:
        send(
            x_all.at[z, c], x_all.at[z, c], xz_s.at[slot(o)], xz_r.at[slot(o)],
            at_tp(z_at(-o), l, c),
        )

    def block_in(o):
        zz = z_at(o)
        arrived(x_all.at[zz, c], xz_s.at[slot(o)], xz_r.at[slot(o)], at_tp(zz, l, c))
        send(
            x_all.at[zz, c], x_all.at[zz, c], xc_s.at[slot(o)], xc_r.at[slot(o)],
            at_tp(z, l, other_c),
        )

    def block_whole(o):
        zz = z_at(o)
        arrived(x_all.at[zz, other_c], xc_s.at[slot(o)], xc_r.at[slot(o)], at_tp(z, l, other_c))

    right, left = at_x(xr), at_x(xl)

    def stage_in(q):
        for o in CHUNKS[q]:
            if o:
                block_in(o)

    def stage_a(q):
        for o in CHUNKS[q]:
            block_whole(o)
        rows = jnp.concatenate(
            [x_all[z_at(o)].reshape(128, 512) for o in CHUNKS[q]], axis=0
        )
        for weight, dst in ((gate_v, gate_p), (up_v, up_p)):
            value = jnp.dot(rows, weight[...], preferred_element_type=F32).astype(BF)
            value = value.reshape(2, NX, 2, 16, 512)
            for b in range(2):
                dst[q, :, 2 * b : 2 * b + 2] = value[b]
        send(gate_p.at[q, xo], m1g.at[q], xp_s.at[q, 0], xp_r.at[q, 0], right)
        send(up_p.at[q, xo], m1u.at[q], xp_s.at[q, 1], xp_r.at[q, 1], left)
        send(up_p.at[q, xr], m2u.at[q], xp_s.at[q, 2], xp_r.at[q, 2], right)
        send(gate_p.at[q, xl], m2g.at[q], xp_s.at[q, 3], xp_r.at[q, 3], left)

    def stage_b(q):
        arrived(m1g.at[q], xp_s.at[q, 0], xp_r.at[q, 0], left)
        s3g[q] = (gate_p[q, xr].astype(F32) + m1g[q].astype(F32)).astype(BF)
        send(s3g.at[q], m3g.at[q], xp_s.at[q, 4], xp_r.at[q, 4], right)
        arrived(m1u.at[q], xp_s.at[q, 1], xp_r.at[q, 1], right)
        s3u[q] = (up_p[q, xl].astype(F32) + m1u[q].astype(F32)).astype(BF)
        send(s3u.at[q], m3u.at[q], xp_s.at[q, 5], xp_r.at[q, 5], left)

    def stage_c(q):
        arrived(m2u.at[q], xp_s.at[q, 2], xp_r.at[q, 2], left)
        arrived(m2g.at[q], xp_s.at[q, 3], xp_r.at[q, 3], right)
        arrived(m3g.at[q], xp_s.at[q, 4], xp_r.at[q, 4], left)
        arrived(m3u.at[q], xp_s.at[q, 5], xp_r.at[q, 5], right)
        gate = gate_p[q, x].astype(F32) + m2g[q].astype(F32) + m3g[q].astype(F32)
        up = up_p[q, x].astype(F32) + m2u[q].astype(F32) + m3u[q].astype(F32)
        h_send[q, :, 0] = gate.astype(BF)
        h_send[q, :, 1] = up.astype(BF)
        for o in range(1, NH):
            place = lax.rem(h + o, NH)
            send(
                h_send.at[q, place], h_recv.at[q, o - 1],
                hp_s.at[q, o - 1], hp_r.at[q, o - 1], at_h(place),
            )

    def stage_d(q):
        for o in range(1, NH):
            arrived(
                h_recv.at[q, o - 1], hp_s.at[q, o - 1], hp_r.at[q, o - 1],
                at_h(lax.rem(h + NH - o, NH)),
            )
        total = h_send[q, h].astype(F32)
        for o in range(NH - 1):
            total = total + h_recv[q, o].astype(F32)
        gate, up = total[0], total[1]
        hid[q, x, h] = (gate / (1.0 + jnp.exp(-gate)) * up).astype(BF)
        for o in range(1, NH):
            send(
                hid.at[q, x, h], hid.at[q, x, h],
                hg_s.at[q, o - 1], hg_r.at[q, o - 1], at_h(lax.rem(h + o, NH)),
            )

    def stage_e(q):
        for o in range(1, NH):
            place = lax.rem(h + NH - o, NH)
            arrived(hid.at[q, x, place], hg_s.at[q, o - 1], hg_r.at[q, o - 1], at_h(place))
        send(hid.at[q, x], hid.at[q, x], xg_s.at[q, 0], xg_r.at[q, 0], right)
        send(hid.at[q, x], hid.at[q, x], xg_s.at[q, 1], xg_r.at[q, 1], left)

    def stage_f(q):
        arrived(hid.at[q, xl], xg_s.at[q, 0], xg_r.at[q, 0], left)
        half = hid.at[q, xl, pl.ds(0, 2)]
        send(half, half, xg_s.at[q, 2], xg_r.at[q, 2], right)
        arrived(hid.at[q, xr], xg_s.at[q, 1], xg_r.at[q, 1], right)
        half = hid.at[q, xr, pl.ds(2, 2)]
        send(half, half, xg_s.at[q, 3], xg_r.at[q, 3], left)

    def stage_g(q):
        arrived(hid.at[q, xo, pl.ds(0, 2)], xg_s.at[q, 2], xg_r.at[q, 2], left)
        arrived(hid.at[q, xo, pl.ds(2, 2)], xg_s.at[q, 3], xg_r.at[q, 3], right)
        rows = jnp.concatenate(
            [hid[q, :, 2 * b : 2 * b + 2].reshape(128, 512) for b in range(2)], axis=0
        )
        value = jnp.dot(rows, down_v[...], preferred_element_type=F32).astype(BF)
        value = value.reshape(2, 2, 2, 32, 512)
        for b in range(2):
            part[q, :, b] = value[b]
        send(part.at[q, other_c], part_in.at[q], oc_s.at[q], oc_r.at[q], at_tp(z, l, other_c))

    def stage_h(q):
        arrived(part_in.at[q], oc_s.at[q], oc_r.at[q], at_tp(z, l, other_c))
        z_send[q] = (part[q, c].astype(F32) + part_in[q].astype(F32)).astype(BF)
        for b, o in enumerate(CHUNKS[q]):
            if o:
                send(
                    z_send.at[q, b], z_recv.at[slot(o)], oz_s.at[slot(o)], oz_r.at[slot(o)],
                    at_tp(z_at(o), l, c),
                )

    stages = (stage_a, stage_b, stage_c, stage_d, stage_e, stage_f, stage_g, stage_h)
    stage_in(0)
    loads[1].wait()
    loads[2].wait()
    count, skew = len(CHUNKS), 2
    for step in range(skew * (count - 1) + len(stages)):
        for q in range(count):
            s = step - skew * q
            if 0 <= s < len(stages):
                if s == 0 and q:
                    pass
                if s == 6 and q == 0:
                    loads[3].wait()
                stages[s](q)
                if s == 0 and q + 1 < count:
                    stage_in(q + 1)

    total = z_send[0, 0].astype(F32)
    for o in offsets[1:]:
        arrived(z_recv.at[slot(o)], oz_s.at[slot(o)], oz_r.at[slot(o)], at_tp(z_at(-o), l, c))
        total = total + z_recv[slot(o)].astype(F32)
    l_send[...] = total.astype(BF)
    send(l_send.at[other_l], l_recv, ol_s, ol_r, at_tp(z, other_l, c))
    arrived(l_recv, ol_s, ol_r, at_tp(z, other_l, c))
    ffn = l_send[l].astype(F32) + l_recv[...].astype(F32)
    for i in range(4):
        tiles[pl.ds(i, 32, stride=4), :] = ffn[:, i * HD : (i + 1) * HD]
    finished = tiles[...].reshape(DP, 8, HD) + spread_c[:, 8:].astype(F32)
    e_recv[...] = finished
    upper_tile = lax.broadcasted_iota(jnp.int32, (8, HD), 0) < 4
    for rank in range(DP):
        e_send[rank] = jnp.where(upper_tile, e_recv[rank], e_recv[plan[2 * MIG + rank]])
    for o, rank in enumerate(others):
        send(e_send.at[rank], out.at[dp], e_s.at[o], e_r.at[o], at_dp(rank))
    out[dp] = e_send[dp]
    exchanged(out, e_s, e_r)
    for copy in sent:
        copy.wait_send()


def on_device(
    queries, residual, new_entries, page_pool, page_table, cache_lengths, migration,
    norm_gain, gate_weight, up_weight, down_weight,
):
    entries = migration[0]
    slot_id = entries[0, 0]
    second = slot_id == 1

    def ordered(value):
        return jnp.where(second, value, value[::-1])

    heads = ordered(queries[0, 0].reshape(2, DP, 4, HD))
    rest = ordered(residual[0, 0].reshape(2, DP, 4, HD))
    fresh = ordered(new_entries[0, 0].reshape(2, DP, 1, HD))
    blank = jnp.zeros((DP, 7, HD), BF)
    own = jnp.stack(
        [
            jnp.concatenate([heads[0], rest[0], fresh[0], blank], axis=1),
            jnp.concatenate([rest[1], heads[1], fresh[1], blank], axis=1),
        ]
    )
    table = ordered(page_table[0, 0])
    lengths = ordered(cache_lengths[0, 0])
    pages, page_rows = page_pool.shape[2], page_pool.shape[3]
    places = jnp.arange(table.shape[1], dtype=jnp.int32)
    held = jnp.clip(lengths[:, None] - page_rows * places[None, :], 0, page_rows)
    match = table[:, :, None] == jnp.arange(pages, dtype=jnp.int32)
    filled = jnp.sum(jnp.where(match, held[:, :, None], 0), axis=1)
    seen = jnp.arange(page_rows, dtype=jnp.int32)[None, None, :] < filled[:, :, None]
    bias = jnp.where(seen, 0.0, -1e30).astype(F32).reshape(1, 2, 1, pages * page_rows)
    bias = jnp.broadcast_to(bias, (2, 2, 4, pages * page_rows)).reshape(16, -1)
    gain = norm_gain.astype(F32).reshape(DP, 1, 4, HD)
    gain = jnp.broadcast_to(gain, (DP, 2, 4, HD)).reshape(DP, 8, HD)
    ranks = jnp.arange(DP, dtype=jnp.int32)
    anchors = ranks
    for i in range(MIG):
        anchors = jnp.where(ranks == entries[i, 2], entries[i, 1], anchors)
    plan = jnp.concatenate([entries[:, 2], entries[:, 1], anchors])

    vmem = pl.BlockSpec(memory_space=pltpu.VMEM)
    hbm = pl.BlockSpec(memory_space=pl.ANY)
    smem = pl.BlockSpec(memory_space=pltpu.SMEM)
    nq = len(CHUNKS)
    dma = pltpu.SemaphoreType.DMA
    share = (nq, NH, 16, 512)
    scratch = [
        pltpu.VMEM((512, 2048), BF),
        pltpu.VMEM((512, 512), BF), pltpu.VMEM((512, 512), BF), pltpu.VMEM((512, 512), BF),
        pltpu.VMEM((DP, 16, HD), BF), pltpu.VMEM((32, HD), BF), pltpu.VMEM((DP, 32, HD), BF),
        pltpu.VMEM((DP, 16, HD), BF), pltpu.VMEM((DP, 16, HD), BF),
        pltpu.VMEM((DP * 8, HD), F32),
        pltpu.VMEM((NZ, 2, 2, 32, 512), BF),
        pltpu.VMEM((nq, NX, NH, 16, 512), BF), pltpu.VMEM((nq, NX, NH, 16, 512), BF),
    ]
    scratch += [pltpu.VMEM(share, BF) for _ in range(8)]
    scratch += [
        pltpu.VMEM((nq, NH, 2, 16, 512), BF), pltpu.VMEM((nq, NH - 1, 2, 16, 512), BF),
        pltpu.VMEM((nq, NX, NH, 16, 512), BF),
        pltpu.VMEM((nq, 2, 2, 2, 32, 512), BF), pltpu.VMEM((nq, 2, 2, 32, 512), BF),
        pltpu.VMEM((nq, 2, 2, 32, 512), BF), pltpu.VMEM((NZ, 2, 32, 512), BF),
        pltpu.VMEM((2, 32, 512), BF), pltpu.VMEM((32, 512), BF),
        pltpu.VMEM((DP, 8, HD), F32), pltpu.VMEM((DP, 8, HD), F32),
    ]
    scratch += [dma((4,))]
    scratch += [dma((DP - 1,)) for _ in range(8)]
    scratch += [dma, dma, dma((NZ,)), dma((NZ,)), dma((NZ,)), dma((NZ,))]
    scratch += [dma((nq, 6)), dma((nq, 6)), dma((nq, 3)), dma((nq, 3)), dma((nq, 3)), dma((nq, 3))]
    scratch += [dma((nq, 4)), dma((nq, 4)), dma((nq,)), dma((nq,)), dma((NZ,)), dma((NZ,)), dma, dma]
    done = pl.pallas_call(
        kernel,
        out_shape=jax.ShapeDtypeStruct((DP, 8, HD), F32),
        in_specs=[smem, vmem, vmem, vmem, hbm, hbm, hbm, hbm],
        out_specs=vmem,
        scratch_shapes=scratch,
        compiler_params=pltpu.CompilerParams(
            collective_id=0, has_side_effects=True, vmem_limit_bytes=50 * 1024 * 1024
        ),
    )(
        plan, own, bias, gain, page_pool.reshape(pages * page_rows, page_pool.shape[4]),
        gate_weight, up_weight, down_weight,
    )
    done = jnp.where(second, done.reshape(DP, 2, 4, HD), done.reshape(DP, 2, 4, HD)[:, ::-1])
    return done.transpose(1, 0, 2, 3).astype(BF).reshape(1, 1, 2, DP * 4 * HD)


def solution(mesh):
    return jax.shard_map(
        on_device,
        mesh=mesh,
        in_specs=(
            P("dp", "tp", None, None),
            P("dp", "tp", None, None),
            P("dp", "tp", None, None),
            P("dp", "tp", None, None, None),
            P("dp", "tp", None, None),
            P("dp", "tp", None),
            P("tp", None, None),
            P(),
            P("dp", "tp"),
            P("dp", "tp"),
            P("tp", "dp"),
        ),
        out_specs=P("dp", "tp", None, None),
        check_vma=False,
    )
```

```python
import math

import jax
import jax.numpy as jnp
from jax import lax
from jax.experimental import pallas as pl
from jax.experimental.pallas import tpu as pltpu
from jax.sharding import PartitionSpec as P

HD = 128
KVH = 8
NX, NH, NZ = 4, 4, 8
DP = NX * NH
MIG = 3
MAXP, PG = 16, 16
NEAR, FAR = (0, 1, -1, 2), (-2, -3, 3, 4)
CHUNKS = ((0, NEAR), (0, FAR), (1, FAR), (1, NEAR))
ORDER = (
    ("local", 0), ("x", 0), ("route", 0), ("y", 0), ("near", 0), ("a", 0), ("listed", 0),
    ("far", 0), ("b", 0), ("x", 1), ("a", 1), ("c", 0), ("y", 1), ("b", 1), ("far", 1), ("c", 1),
    ("a", 2), ("d", 0), ("near", 1), ("b", 2), ("a", 3), ("d", 1), ("c", 2), ("b", 3), ("e", 0),
    ("e", 1), ("c", 3), ("f", 0), ("d", 2), ("f", 1), ("g", 0), ("d", 3), ("g", 1), ("e", 2),
    ("h", 0), ("h", 1), ("f", 2), ("e", 3), ("g", 2), ("f", 3), ("h", 2), ("g", 3), ("h", 3),
)
EPSILON = 1e-05
BF = jnp.bfloat16
F32 = jnp.float32


def kernel(
    mig, table, lengths, q_in, res_in, new_in, gain, pool, gate_w, up_w, down_w, out,
    pool_v, gate_v, up_v, down_v,
    q_t, res_t, new_t, own, line, y_send, y_recv, c_send, spread_c, tiles, x_all,
    gate_p, up_p, m1g, m1u, m2g, m2u, s3g, s3u, m3g, m3u,
    h_send, h_recv, hid, part, part_in, z_send, z_recv, l_send, l_recv,
    fin, e_send, e_recv,
    load_sem, rx_s, rx_r, ry_s, ry_r, c_s, c_r, e_s, e_r,
    xl_s, xl_r, xz_s, xz_r, xc_s, xc_r,
    xp_s, xp_r, hp_s, hp_r, hg_s, hg_r, xg_s, xg_r,
    oc_s, oc_r, oz_s, oz_r, ol_s, ol_r,
):
    dp, tp = lax.axis_index("dp"), lax.axis_index("tp")
    h, x = lax.div(dp, NX), lax.rem(dp, NX)
    z, low = lax.div(tp, 4), lax.rem(tp, 4)
    l, c = lax.div(low, 2), lax.rem(low, 2)
    other_l, other_c = 1 - l, 1 - c
    xr, xo, xl = lax.rem(x + 1, NX), lax.rem(x + 2, NX), lax.rem(x + 3, NX)
    right, left = (h * NX + xr, tp), (h * NX + xl, tp)

    def at_dp(rank):
        return (rank, tp)

    def at_h(place):
        return (place * NX + x, tp)

    def at_tp(zz, ll, cc):
        return (dp, zz * 4 + ll * 2 + cc)

    def z_at(offset):
        return lax.rem(z + (offset + NZ), NZ)

    def slot(offset):
        return (offset + NZ) % NZ

    across_l, across_c = at_tp(z, other_l, c), at_tp(z, l, other_c)
    sent = []

    def send(src, dst, send_sem, recv_sem, device, listed_copy=True):
        copy = pltpu.make_async_remote_copy(
            src_ref=src, dst_ref=dst, send_sem=send_sem, recv_sem=recv_sem,
            device_id=device, device_id_type=pl.DeviceIdType.MESH,
        )
        copy.start()
        if listed_copy:
            sent.append(copy)

    def arrived(dst, send_sem, recv_sem, device):
        pltpu.make_async_remote_copy(
            src_ref=dst, dst_ref=dst, send_sem=send_sem, recv_sem=recv_sem,
            device_id=device, device_id_type=pl.DeviceIdType.MESH,
        ).wait_recv()

    loads = [
        pltpu.make_async_copy(src, dst, load_sem.at[i])
        for i, (src, dst) in enumerate(
            ((pool, pool_v), (gate_w, gate_v), (up_w, up_v), (down_w, down_v))
        )
    ]
    for copy in loads:
        copy.start()

    others = [lax.rem(dp + o, DP) for o in range(1, DP)]
    barrier = pltpu.get_barrier_semaphore()
    partners = [at_dp(rank) for rank in others]
    partners += [at_tp(z_at(o), l, c) for o in range(1, NZ)] + [across_l, across_c]
    for device in partners:
        pl.semaphore_signal(barrier, inc=1, device_id=device, device_id_type=pl.DeviceIdType.MESH)

    def exchange(src, dst, s_sem, r_sem):
        for rank in others:
            send(src.at[rank], dst.at[dp], s_sem, r_sem, at_dp(rank), False)
        dst[dp] = src[dp]

    def exchanged(dst, s_sem, r_sem):
        arrived(dst.at[pl.ds(0, DP - 1)], s_sem, r_sem, at_dp(others[0]))

    def all_left(src, s_sem, r_sem):
        part = src.at[pl.ds(0, DP - 1)]
        pltpu.make_async_remote_copy(
            src_ref=part, dst_ref=part, send_sem=s_sem, recv_sem=r_sem,
            device_id=at_dp(others[0]), device_id_type=pl.DeviceIdType.MESH,
        ).wait_send()

    slot_id = mig[0, 0]
    second = slot_id == 1

    def ordered(value):
        return jnp.where(second, value, jnp.concatenate([value[1:2], value[0:1]], axis=0))

    for source, dst, count in ((q_in, q_t, 64), (res_in, res_t, 64), (new_in, new_t, 16)):
        value = ordered(source[...].astype(F32))
        for j in range(count):
            dst[pl.ds(j, 2, stride=count), :] = value[:, j * HD : (j + 1) * HD]

    top_half = lax.broadcasted_iota(jnp.int32, (KVH, 8, HD), 1) < 4

    def turned(value):
        return jnp.concatenate([value[:, 4:], value[:, :4]], axis=1)

    def pieces(first, second_value):
        even = jnp.where(top_half, first, turned(second_value))
        odd = jnp.where(top_half, turned(first), second_value)
        return even, odd

    own[...] = jnp.concatenate([q_t[64:], res_t[64:], new_t[16:]], axis=0).astype(BF)

    def bias_of(place):
        lane = lax.broadcasted_iota(jnp.int32, (8, MAXP * 2 * PG), 1)
        page, inner = lane // PG, lane % PG
        length = lengths[place]
        filled = jnp.zeros_like(lane)
        for p in range(MAXP):
            held = jnp.minimum(jnp.maximum(length - p * PG, 0), PG)
            filled = jnp.where(page == table[place, p], held, filled)
        return jnp.where(inner < filled, 0.0, -1e30)

    def attend(w, q_rows, res_rows, new_rows, hidden_bias):
        factor = 1.0 / math.sqrt(HD)
        new_keys = jnp.stack([new_rows[j : j + 1] for j in range(KVH)])
        new_values = jnp.stack([new_rows[KVH + j : KVH + j + 1] for j in range(KVH)])
        q_bf = q_rows.astype(BF)
        score = jnp.stack(
            [
                lax.dot_general(
                    q_bf[head], pool_v[:, head * HD : (head + 1) * HD],
                    (((1,), (1,)), ((), ())), preferred_element_type=F32,
                )
                for head in range(KVH)
            ]
        )
        score = score * factor + hidden_bias[None]
        own_score = jnp.sum(q_rows * new_keys, axis=-1, keepdims=True) * factor
        top = jnp.maximum(jnp.max(score, axis=-1, keepdims=True), own_score)
        exponent = jnp.exp(score - top)
        own_exponent = jnp.exp(own_score - top)
        scale = 1.0 / (jnp.sum(exponent, axis=-1, keepdims=True) + own_exponent)
        weight = (exponent * scale).astype(BF)
        own_weight = (own_exponent * scale).astype(BF).astype(F32)
        attended = jnp.stack(
            [
                jnp.dot(
                    weight[head], pool_v[:, (KVH + head) * HD : (KVH + head + 1) * HD],
                    preferred_element_type=F32,
                )
                for head in range(KVH)
            ]
        )
        stream = res_rows + attended + own_weight * new_values
        square = jnp.sum(jnp.sum(stream * stream, axis=0), axis=-1, keepdims=True)
        mean = jnp.sum(square, axis=0, keepdims=True) * (1.0 / (DP * 4 * HD))
        scale = lax.rsqrt(mean + EPSILON)
        normed = stream * scale[None] * gain[...].astype(F32).reshape(KVH, 8, HD)
        even, odd = pieces(normed, stream)
        for k in range(DP):
            c_send[w, k] = (even, odd)[k % 2][k // 2]

    def spread(w):
        exchange(c_send.at[w], spread_c.at[w], c_s.at[w], c_r.at[w])

    def local(_):
        local_q = q_t[:64].reshape(KVH, 8, HD)
        local_res = res_t[:64].reshape(KVH, 8, HD)
        hidden_bias = bias_of(1 - slot_id)
        loads[0].wait()
        attend(0, local_q, local_res, new_t[:16], hidden_bias)
        pl.semaphore_wait(barrier, len(partners))
        spread(0)
        for o in range(1, NX):
            send(
                own, line.at[x], rx_s.at[o - 1], rx_r.at[o - 1],
                (h * NX + lax.rem(x + o, NX), tp),
            )
        line[x] = own[...]

    sources = [mig[i, 1] for i in range(MIG)]
    targets = [mig[i, 2] for i in range(MIG)]

    def route(_):
        for o in range(1, NX):
            place = lax.rem(x + NX - o, NX)
            arrived(line.at[place], rx_s.at[o - 1], rx_r.at[o - 1], (h * NX + place, tp))
        rows = [line[lax.rem(target, NX)].astype(F32) for target in targets]
        here = [lax.div(target, NX) == h for target in targets]

        def wanted(rank):
            value = jnp.zeros_like(rows[0])
            for i in range(MIG):
                value = jnp.where(here[i] & (sources[i] == rank), rows[i], value)
            return value.astype(BF)

        for o in range(1, NH):
            place = lax.rem(h + o, NH)
            y_send[o - 1] = wanted(place * NX + x)
            send(
                y_send.at[o - 1], y_recv.at[o - 1], ry_s.at[o - 1], ry_r.at[o - 1], at_h(place)
            )
        y_recv[NH - 1] = wanted(dp)

    def listed(_):
        for o in range(1, NH):
            arrived(
                y_recv.at[o - 1], ry_s.at[o - 1], ry_r.at[o - 1], at_h(lax.rem(h + NH - o, NH))
            )
        routed = y_recv[NH - 1].astype(F32)
        for o in range(NH - 1):
            routed = routed + y_recv[o].astype(F32)
        serves = (sources[0] == dp) | (sources[1] == dp) | (sources[2] == dp)
        row = jnp.where(serves, routed, own[...].astype(F32))
        attend(
            1, row[:64].reshape(KVH, 8, HD), row[64:128].reshape(KVH, 8, HD), row[128:],
            bias_of(slot_id),
        )
        spread(1)

    def start_x(w):
        exchanged(spread_c.at[w], c_s.at[w], c_r.at[w])
        tiles[...] = spread_c[w].reshape(DP * 8, HD)
        x_all[w, z, c, l] = jnp.concatenate(
            [tiles[pl.ds(i, DP, stride=8), :] for i in range(4)], axis=1
        ).astype(BF)
        block = x_all.at[w, z, c, l]
        send(block, block, xl_s.at[w], xl_r.at[w], across_l)

    def start_y(w):
        arrived(x_all.at[w, z, c, other_l], xl_s.at[w], xl_r.at[w], across_l)
        block = x_all.at[w, z, c]
        send(block, block, xc_s.at[w, 0], xc_r.at[w, 0], across_c)
        offsets = NEAR[1:] + FAR if w == 0 else FAR + NEAR[1:]
        for o in offsets:
            send(block, block, xz_s.at[w, slot(o)], xz_r.at[w, slot(o)], at_tp(z_at(-o), l, c))

    def forward(offsets):
        def run(w):
            for o in offsets:
                if o:
                    zz = z_at(o)
                    block = x_all.at[w, zz, c]
                    arrived(block, xz_s.at[w, slot(o)], xz_r.at[w, slot(o)], at_tp(zz, l, c))
                    send(block, block, xc_s.at[w, slot(o)], xc_r.at[w, slot(o)], across_c)

        return run

    def stage_a(q):
        w, offsets = CHUNKS[q]
        for o in offsets:
            arrived(x_all.at[w, z_at(o), other_c], xc_s.at[w, slot(o)], xc_r.at[w, slot(o)], across_c)
        if q == 0:
            loads[1].wait()
            loads[2].wait()
        rows = jnp.concatenate([x_all[w, z_at(o)].reshape(64, 512) for o in offsets], axis=0)
        for weight, dst in ((gate_v, gate_p), (up_v, up_p)):
            value = jnp.dot(rows, weight[...], preferred_element_type=F32).astype(BF)
            value = value.reshape(NH, NX, 16, 512)
            for b in range(NH):
                dst[q, :, b] = value[b]
        send(gate_p.at[q, xo], m1g.at[q], xp_s.at[q, 0], xp_r.at[q, 0], right)
        send(up_p.at[q, xo], m1u.at[q], xp_s.at[q, 1], xp_r.at[q, 1], left)
        send(up_p.at[q, xr], m2u.at[q], xp_s.at[q, 2], xp_r.at[q, 2], right)
        send(gate_p.at[q, xl], m2g.at[q], xp_s.at[q, 3], xp_r.at[q, 3], left)

    def stage_b(q):
        arrived(m1g.at[q], xp_s.at[q, 0], xp_r.at[q, 0], left)
        s3g[q] = (gate_p[q, xr].astype(F32) + m1g[q].astype(F32)).astype(BF)
        send(s3g.at[q], m3g.at[q], xp_s.at[q, 4], xp_r.at[q, 4], right)
        arrived(m1u.at[q], xp_s.at[q, 1], xp_r.at[q, 1], right)
        s3u[q] = (up_p[q, xl].astype(F32) + m1u[q].astype(F32)).astype(BF)
        send(s3u.at[q], m3u.at[q], xp_s.at[q, 5], xp_r.at[q, 5], left)

    def stage_c(q):
        arrived(m2u.at[q], xp_s.at[q, 2], xp_r.at[q, 2], left)
        arrived(m2g.at[q], xp_s.at[q, 3], xp_r.at[q, 3], right)
        arrived(m3g.at[q], xp_s.at[q, 4], xp_r.at[q, 4], left)
        arrived(m3u.at[q], xp_s.at[q, 5], xp_r.at[q, 5], right)
        gate = gate_p[q, x].astype(F32) + m2g[q].astype(F32) + m3g[q].astype(F32)
        up = up_p[q, x].astype(F32) + m2u[q].astype(F32) + m3u[q].astype(F32)
        h_send[q, :, 0] = gate.astype(BF)
        h_send[q, :, 1] = up.astype(BF)
        for o in range(1, NH):
            place = lax.rem(h + o, NH)
            send(
                h_send.at[q, place], h_recv.at[q, o - 1],
                hp_s.at[q, o - 1], hp_r.at[q, o - 1], at_h(place),
            )

    def stage_d(q):
        for o in range(1, NH):
            arrived(
                h_recv.at[q, o - 1], hp_s.at[q, o - 1], hp_r.at[q, o - 1],
                at_h(lax.rem(h + NH - o, NH)),
            )
        total = h_send[q, h].astype(F32)
        for o in range(NH - 1):
            total = total + h_recv[q, o].astype(F32)
        gate, up = total[0], total[1]
        hid[q, x, h] = (gate / (1.0 + jnp.exp(-gate)) * up).astype(BF)
        for o in range(1, NH):
            send(
                hid.at[q, x, h], hid.at[q, x, h],
                hg_s.at[q, o - 1], hg_r.at[q, o - 1], at_h(lax.rem(h + o, NH)),
            )

    def stage_e(q):
        for o in range(1, NH):
            place = lax.rem(h + NH - o, NH)
            arrived(hid.at[q, x, place], hg_s.at[q, o - 1], hg_r.at[q, o - 1], at_h(place))
        send(hid.at[q, x], hid.at[q, x], xg_s.at[q, 0], xg_r.at[q, 0], right)
        send(hid.at[q, x], hid.at[q, x], xg_s.at[q, 1], xg_r.at[q, 1], left)

    def stage_f(q):
        arrived(hid.at[q, xl], xg_s.at[q, 0], xg_r.at[q, 0], left)
        half = hid.at[q, xl, pl.ds(0, 2)]
        send(half, half, xg_s.at[q, 2], xg_r.at[q, 2], right)
        arrived(hid.at[q, xr], xg_s.at[q, 1], xg_r.at[q, 1], right)
        half = hid.at[q, xr, pl.ds(2, 2)]
        send(half, half, xg_s.at[q, 3], xg_r.at[q, 3], left)

    def stage_g(q):
        arrived(hid.at[q, xo, pl.ds(0, 2)], xg_s.at[q, 2], xg_r.at[q, 2], left)
        arrived(hid.at[q, xo, pl.ds(2, 2)], xg_s.at[q, 3], xg_r.at[q, 3], right)
        if q == 0:
            loads[3].wait()
        rows = jnp.concatenate([hid[q, :, b].reshape(64, 512) for b in range(NH)], axis=0)
        value = jnp.dot(rows, down_v[...], preferred_element_type=F32).astype(BF)
        value = value.reshape(NH, 2, 2, 16, 512)
        for b in range(NH):
            part[q, :, b] = value[b]
        send(part.at[q, other_c], part_in.at[q], oc_s.at[q], oc_r.at[q], across_c)

    def stage_h(q):
        w, offsets = CHUNKS[q]
        arrived(part_in.at[q], oc_s.at[q], oc_r.at[q], across_c)
        z_send[q] = (part[q, c].astype(F32) + part_in[q].astype(F32)).astype(BF)
        for b, o in enumerate(offsets):
            if o:
                send(
                    z_send.at[q, b], z_recv.at[w, slot(o)],
                    oz_s.at[w, slot(o)], oz_r.at[w, slot(o)], at_tp(z_at(o), l, c),
                )

    steps = {
        "local": local, "route": route, "listed": listed, "x": start_x, "y": start_y,
        "near": forward(NEAR), "far": forward(FAR), "a": stage_a, "b": stage_b, "c": stage_c,
        "d": stage_d, "e": stage_e, "f": stage_f, "g": stage_g, "h": stage_h,
    }
    for name, which in ORDER:
        steps[name](which)

    for w, q in ((0, 0), (1, 3)):
        total = z_send[q, 0].astype(F32)
        for o in FAR + NEAR[1:]:
            arrived(
                z_recv.at[w, slot(o)], oz_s.at[w, slot(o)], oz_r.at[w, slot(o)],
                at_tp(z_at(-o), l, c),
            )
            total = total + z_recv[w, slot(o)].astype(F32)
        l_send[:, w] = total.astype(BF)
    send(l_send.at[other_l], l_recv, ol_s, ol_r, across_l)
    arrived(l_recv, ol_s, ol_r, across_l)
    for w in range(2):
        ffn = l_send[l, w].astype(F32) + l_recv[w].astype(F32)
        for i in range(4):
            tiles[pl.ds(4 * w + i, DP, stride=8), :] = ffn[:, i * HD : (i + 1) * HD]
    first = lax.broadcasted_iota(jnp.int32, (DP, 8, HD), 1) < 4
    fin[...] = tiles[...].reshape(DP, 8, HD) + jnp.where(first, turned(spread_c[0]), spread_c[1])
    for rank in range(DP):
        anchor = jnp.int32(rank)
        for i in range(MIG):
            anchor = jnp.where(mig[i, 2] == rank, mig[i, 1], anchor)
        e_send[rank] = jnp.where(first[0], fin[rank], fin[anchor])
    exchange(e_send, e_recv, e_s, e_r)
    for w in range(2):
        all_left(c_send.at[w], c_s.at[w], c_r.at[w])
    for copy in sent:
        copy.wait_send()
    exchanged(e_recv, e_s, e_r)
    tiles[...] = e_recv[...].reshape(DP * 8, HD)
    value = jnp.concatenate(
        [tiles[pl.ds(k * 8 + i, 2, stride=4), :] for k in range(DP) for i in range(4)], axis=1
    )
    out[...] = ordered(value).astype(BF)
    all_left(e_send, e_s, e_r)


def on_device(
    queries, residual, new_entries, page_pool, page_table, cache_lengths, migration,
    norm_gain, gate_weight, up_weight, down_weight,
):
    pages, page_rows, entry = page_pool.shape[2:]
    vmem = pl.BlockSpec(memory_space=pltpu.VMEM)
    hbm = pl.BlockSpec(memory_space=pl.ANY)
    smem = pl.BlockSpec(memory_space=pltpu.SMEM)
    nq = len(CHUNKS)
    dma = pltpu.SemaphoreType.DMA
    share = (nq, NH, 16, 512)
    scratch = [
        pltpu.VMEM((512, 2048), BF),
        pltpu.VMEM((512, 512), BF), pltpu.VMEM((512, 512), BF), pltpu.VMEM((512, 512), BF),
        pltpu.VMEM((128, HD), F32), pltpu.VMEM((128, HD), F32), pltpu.VMEM((32, HD), F32),
        pltpu.VMEM((144, HD), BF), pltpu.VMEM((NX, 144, HD), BF),
        pltpu.VMEM((NH - 1, 144, HD), BF), pltpu.VMEM((NH, 144, HD), BF),
        pltpu.VMEM((2, DP, 8, HD), F32), pltpu.VMEM((2, DP, 8, HD), F32),
        pltpu.VMEM((DP * 8, HD), F32),
        pltpu.VMEM((2, NZ, 2, 2, 16, 512), BF),
        pltpu.VMEM((nq, NX, NH, 16, 512), BF), pltpu.VMEM((nq, NX, NH, 16, 512), BF),
    ]
    scratch += [pltpu.VMEM(share, BF) for _ in range(8)]
    scratch += [
        pltpu.VMEM((nq, NH, 2, 16, 512), BF), pltpu.VMEM((nq, NH - 1, 2, 16, 512), BF),
        pltpu.VMEM((nq, NX, NH, 16, 512), BF),
        pltpu.VMEM((nq, 2, NH, 2, 16, 512), BF), pltpu.VMEM((nq, NH, 2, 16, 512), BF),
        pltpu.VMEM((nq, NH, 2, 16, 512), BF), pltpu.VMEM((2, NZ, 2, 16, 512), BF),
        pltpu.VMEM((2, 2, 16, 512), BF), pltpu.VMEM((2, 16, 512), BF),
        pltpu.VMEM((DP, 8, HD), F32), pltpu.VMEM((DP, 8, HD), F32), pltpu.VMEM((DP, 8, HD), F32),
    ]
    scratch += [dma((4,))]
    scratch += [dma((3,)) for _ in range(4)]
    scratch += [dma((2,)), dma((2,)), dma, dma]
    scratch += [dma((2,)), dma((2,)), dma((2, NZ)), dma((2, NZ)), dma((2, NZ)), dma((2, NZ))]
    scratch += [dma((nq, 6)), dma((nq, 6)), dma((nq, 3)), dma((nq, 3)), dma((nq, 3)), dma((nq, 3))]
    scratch += [dma((nq, 4)), dma((nq, 4)), dma((nq,)), dma((nq,)), dma((2, NZ)), dma((2, NZ)), dma, dma]
    done = pl.pallas_call(
        kernel,
        out_shape=jax.ShapeDtypeStruct((2, DP * 4 * HD), BF),
        in_specs=[smem, smem, smem, vmem, vmem, vmem, vmem, hbm, hbm, hbm, hbm],
        out_specs=vmem,
        scratch_shapes=scratch,
        compiler_params=pltpu.CompilerParams(
            collective_id=0, has_side_effects=True, vmem_limit_bytes=62 * 1024 * 1024
        ),
    )(
        migration[0], page_table[0, 0], cache_lengths[0, 0],
        queries[0, 0], residual[0, 0], new_entries[0, 0], norm_gain.reshape(DP * 4, HD),
        page_pool.reshape(pages * page_rows, entry), gate_weight, up_weight, down_weight,
    )
    return done.reshape(1, 1, 2, DP * 4 * HD)


def solution(mesh):
    return jax.shard_map(
        on_device,
        mesh=mesh,
        in_specs=(
            P("dp", "tp", None, None),
            P("dp", "tp", None, None),
            P("dp", "tp", None, None),
            P("dp", "tp", None, None, None),
            P("dp", "tp", None, None),
            P("dp", "tp", None),
            P("tp", None, None),
            P(),
            P("dp", "tp"),
            P("dp", "tp"),
            P("tp", "dp"),
        ),
        out_specs=P("dp", "tp", None, None),
        check_vma=False,
    )
```

```python
import math

import jax
import jax.numpy as jnp
from jax import lax
from jax.experimental import pallas as pl
from jax.experimental.pallas import tpu as pltpu
from jax.sharding import PartitionSpec as P

HD = 128
KVH = 8
NX, NH, NZ = 4, 4, 8
DP = NX * NH
MIG = 3
MAXP, PG = 16, 16
CHUNKS = (
    (0, (0, 1)), (0, (-1, 2)), (0, (-2, 3)), (0, (-3, 4)),
    (1, (-3, 4)), (1, (-2, 3)), (1, (-1, 2)), (1, (0, 1)),
)
SIZES = [16 * len(offsets) for _, offsets in CHUNKS]
STARTS = [sum(SIZES[:q]) for q in range(len(CHUNKS))]
ORDER = (
    "local", "x0", "route", "y0", "w0", "w1", "a0", "listed", "b0", "w2", "a1", "x1", "a2", "w3",
    "b1", "y1", "c0", "a3", "c1", "b2", "b3", "d0", "w4", "w5", "c2", "a4", "w6", "w7", "d1",
    "a5", "c3", "b4", "a7", "d2", "b5", "e0", "c4", "a6", "d3", "e1", "c5", "e2", "b6", "f0",
    "b7", "d4", "f1", "f2", "e3", "c6", "d5", "c7", "g2", "e4", "g0", "g1", "f3", "d6", "h2",
    "e5", "f4", "h0", "g3", "h1", "d7", "e6", "h3", "g4", "f5", "e7", "f6", "h4", "g5", "f7",
    "g6", "h5", "l0", "g7", "h6", "h7", "m0", "l1", "m1",
)
DISTANCES = (10, 9, 11, 8, 6, 14, 2, 5, 7, 13, 15, 4, 12, 1, 3)
EPSILON = 1e-05
BF = jnp.bfloat16
F32 = jnp.float32


def kernel(
    mig, table, lengths, q_in, res_in, new_in, gain, pool, gate_w, up_w, down_w, out,
    pool_v, gate_v, up_v, down_v,
    q_t, res_t, new_t, own, line, y_send, y_recv, c_local, c_listed, in_local, in_listed,
    stream_local, tiles, x_all,
    gate_p, up_p, m1g, m1u, m2g, m2u, s3g, s3u, m3g, m3u,
    h_send, h_recv, hid, part, part_in, z_send, z_recv, l_send, l_recv,
    rows_out, fin, e_send, e_recv,
    load_sem, rx_s, rx_r, ry_s, ry_r, c_s, c_r, e_s, e_r,
    xl_s, xl_r, xz_s, xz_r, xc_s, xc_r,
    xp_s, xp_r, hp_s, hp_r, hg_s, hg_r, xg_s, xg_r,
    oc_s, oc_r, oz_s, oz_r, ol_s, ol_r,
):
    dp, tp = lax.axis_index("dp"), lax.axis_index("tp")
    h, x = lax.div(dp, NX), lax.rem(dp, NX)
    z, low = lax.div(tp, 4), lax.rem(tp, 4)
    l, c = lax.div(low, 2), lax.rem(low, 2)
    other_l, other_c = 1 - l, 1 - c
    xr, xo, xl = lax.rem(x + 1, NX), lax.rem(x + 2, NX), lax.rem(x + 3, NX)
    right, left = (h * NX + xr, tp), (h * NX + xl, tp)

    def at_dp(rank):
        return (rank, tp)

    def at_h(place):
        return (place * NX + x, tp)

    def at_tp(zz, ll, cc):
        return (dp, zz * 4 + ll * 2 + cc)

    def z_at(offset):
        return lax.rem(z + (offset + NZ), NZ)

    def slot(offset):
        return (offset + NZ) % NZ

    across_l, across_c = at_tp(z, other_l, c), at_tp(z, l, other_c)
    sent = []

    def send(src, dst, send_sem, recv_sem, device, listed_copy=True):
        copy = pltpu.make_async_remote_copy(
            src_ref=src, dst_ref=dst, send_sem=send_sem, recv_sem=recv_sem,
            device_id=device, device_id_type=pl.DeviceIdType.MESH,
        )
        copy.start()
        if listed_copy:
            sent.append(copy)

    def arrived(dst, send_sem, recv_sem, device):
        pltpu.make_async_remote_copy(
            src_ref=dst, dst_ref=dst, send_sem=send_sem, recv_sem=recv_sem,
            device_id=device, device_id_type=pl.DeviceIdType.MESH,
        ).wait_recv()

    loads = [
        pltpu.make_async_copy(src, dst, load_sem.at[i])
        for i, (src, dst) in enumerate(
            ((pool, pool_v), (gate_w, gate_v), (up_w, up_v), (down_w, down_v))
        )
    ]
    for copy in loads:
        copy.start()
    waiting = set(range(len(loads)))

    def use(i):
        if i in waiting:
            waiting.discard(i)
            loads[i].wait()


    others = [lax.rem(h + o // NX, NH) * NX + lax.rem(x + o % NX, NX) for o in DISTANCES]
    barrier = pltpu.get_barrier_semaphore()
    partners = [at_dp(rank) for rank in others]
    partners += [at_tp(z_at(o), l, c) for o in range(1, NZ)] + [across_l, across_c]
    for device in partners:
        pl.semaphore_signal(barrier, inc=1, device_id=device, device_id_type=pl.DeviceIdType.MESH)

    def exchange(src, dst, s_sem, r_sem):
        for rank in others:
            send(src.at[rank], dst.at[dp], s_sem, r_sem, at_dp(rank), False)
        dst[dp] = src[dp]

    def exchanged(dst, s_sem, r_sem):
        arrived(dst.at[pl.ds(0, DP - 1)], s_sem, r_sem, at_dp(others[0]))

    def all_left(src, s_sem, r_sem):
        part = src.at[pl.ds(0, DP - 1)]
        pltpu.make_async_remote_copy(
            src_ref=part, dst_ref=part, send_sem=s_sem, recv_sem=r_sem,
            device_id=at_dp(others[0]), device_id_type=pl.DeviceIdType.MESH,
        ).wait_send()

    slot_id = mig[0, 0, 0]
    second = slot_id == 1

    def ordered(value):
        return jnp.where(second, value, jnp.concatenate([value[1:2], value[0:1]], axis=0))

    for source, dst, count in ((q_in, q_t, 64), (res_in, res_t, 64), (new_in, new_t, 16)):
        value = ordered(source[...].astype(F32))
        for j in range(count):
            dst[pl.ds(j, 2, stride=count), :] = value[:, j * HD : (j + 1) * HD]

    top_half = lax.broadcasted_iota(jnp.int32, (KVH, 8, HD), 1) < 4

    def turned(value):
        return jnp.concatenate([value[:, 4:], value[:, :4]], axis=1)

    def pieces(first, second_value):
        even = jnp.where(top_half, first, turned(second_value))
        odd = jnp.where(top_half, turned(first), second_value)
        return even, odd

    own[...] = jnp.concatenate([q_t[64:], res_t[64:], new_t[16:]], axis=0).astype(BF)

    def bias_of(place):
        lane = lax.broadcasted_iota(jnp.int32, (8, MAXP * 2 * PG), 1)
        page, inner = lane // PG, lane % PG
        length = lengths[place]
        filled = jnp.zeros_like(lane)
        for p in range(MAXP):
            held = jnp.minimum(jnp.maximum(length - p * PG, 0), PG)
            filled = jnp.where(page == table[place, p], held, filled)
        return jnp.where(inner < filled, 0.0, -1e30)

    def attend(q_rows, res_rows, new_rows, hidden_bias):
        factor = 1.0 / math.sqrt(HD)
        new_keys = jnp.stack([new_rows[j : j + 1] for j in range(KVH)])
        new_values = jnp.stack([new_rows[KVH + j : KVH + j + 1] for j in range(KVH)])
        q_bf = q_rows.astype(BF)
        score = jnp.stack(
            [
                lax.dot_general(
                    q_bf[head], pool_v[:, head * HD : (head + 1) * HD],
                    (((1,), (1,)), ((), ())), preferred_element_type=F32,
                )
                for head in range(KVH)
            ]
        )
        score = score * factor + hidden_bias[None]
        own_score = jnp.sum(q_rows * new_keys, axis=-1, keepdims=True) * factor
        top = jnp.maximum(jnp.max(score, axis=-1, keepdims=True), own_score)
        exponent = jnp.exp(score - top)
        own_exponent = jnp.exp(own_score - top)
        scale = 1.0 / (jnp.sum(exponent, axis=-1, keepdims=True) + own_exponent)
        weight = (exponent * scale).astype(BF)
        own_weight = (own_exponent * scale).astype(BF).astype(F32)
        attended = jnp.stack(
            [
                jnp.dot(
                    weight[head], pool_v[:, (KVH + head) * HD : (KVH + head + 1) * HD],
                    preferred_element_type=F32,
                )
                for head in range(KVH)
            ]
        )
        stream = res_rows + attended + own_weight * new_values
        square = jnp.sum(jnp.sum(stream * stream, axis=0), axis=-1, keepdims=True)
        mean = jnp.sum(square, axis=0, keepdims=True) * (1.0 / (DP * 4 * HD))
        scale = lax.rsqrt(mean + EPSILON)
        normed = stream * scale[None] * gain[...].astype(F32).reshape(KVH, 8, HD)
        return normed, stream

    def local(_):
        local_q = q_t[:64].reshape(KVH, 8, HD)
        local_res = res_t[:64].reshape(KVH, 8, HD)
        hidden_bias = bias_of(1 - slot_id)
        use(0)
        normed, stream = attend(local_q, local_res, new_t[:16], hidden_bias)
        stream_local[...] = stream.reshape(DP * 4, HD)
        for k in range(DP):
            c_local[k] = normed[k // 2, 4 * (k % 2) : 4 * (k % 2) + 4]
        pl.semaphore_wait(barrier, len(partners))
        exchange(c_local, in_local, c_s.at[0], c_r.at[0])
        for o in range(1, NX):
            send(
                own, line.at[x], rx_s.at[o - 1], rx_r.at[o - 1],
                (h * NX + lax.rem(x + o, NX), tp),
            )
        line[x] = own[...]

    sources = [mig[i, 0, 1] for i in range(MIG)]
    targets = [mig[i, 0, 2] for i in range(MIG)]

    def route(_):
        for o in range(1, NX):
            place = lax.rem(x + NX - o, NX)
            arrived(line.at[place], rx_s.at[o - 1], rx_r.at[o - 1], (h * NX + place, tp))
        rows = [line[lax.rem(target, NX)].astype(F32) for target in targets]
        here = [lax.div(target, NX) == h for target in targets]

        def wanted(rank):
            value = jnp.zeros_like(rows[0])
            for i in range(MIG):
                value = jnp.where(here[i] & (sources[i] == rank), rows[i], value)
            return value.astype(BF)

        for o in range(1, NH):
            place = lax.rem(h + o, NH)
            y_send[o - 1] = wanted(place * NX + x)
            send(
                y_send.at[o - 1], y_recv.at[o - 1], ry_s.at[o - 1], ry_r.at[o - 1], at_h(place)
            )
        y_recv[NH - 1] = wanted(dp)

    def listed(_):
        for o in range(1, NH):
            arrived(
                y_recv.at[o - 1], ry_s.at[o - 1], ry_r.at[o - 1], at_h(lax.rem(h + NH - o, NH))
            )
        routed = y_recv[NH - 1].astype(F32)
        for o in range(NH - 1):
            routed = routed + y_recv[o].astype(F32)
        serves = (sources[0] == dp) | (sources[1] == dp) | (sources[2] == dp)
        row = jnp.where(serves, routed, own[...].astype(F32))
        normed, stream = attend(
            row[:64].reshape(KVH, 8, HD), row[64:128].reshape(KVH, 8, HD), row[128:],
            bias_of(slot_id),
        )
        even, odd = pieces(normed, stream)
        for k in range(DP):
            c_listed[k] = (even, odd)[k % 2][k // 2]
        exchange(c_listed, in_listed, c_s.at[1], c_r.at[1])

    def start_x(w):
        source, count = (in_local, 4) if w == 0 else (in_listed, 8)
        exchanged(source, c_s.at[w], c_r.at[w])
        for a in range(DP):
            tiles[count * a : count * a + count] = source[a]
        x_all[w, z, c, l] = jnp.concatenate(
            [tiles[pl.ds(i, DP, stride=count), :] for i in range(4)], axis=1
        ).astype(BF)
        block = x_all.at[w, z, c, l]
        send(block, block, xl_s.at[w], xl_r.at[w], across_l)

    def start_y(w):
        arrived(x_all.at[w, z, c, other_l], xl_s.at[w], xl_r.at[w], across_l)
        block = x_all.at[w, z, c]
        send(block, block, xc_s.at[w, 0], xc_r.at[w, 0], across_c)
        offsets = [o for kind, places in CHUNKS if kind == w for o in places if o]
        for o in offsets:
            send(block, block, xz_s.at[w, slot(o)], xz_r.at[w, slot(o)], at_tp(z_at(-o), l, c))

    def forward(q):
        w, offsets = CHUNKS[q]
        for o in offsets:
            if o:
                zz = z_at(o)
                block = x_all.at[w, zz, c]
                arrived(block, xz_s.at[w, slot(o)], xz_r.at[w, slot(o)], at_tp(zz, l, c))
                send(block, block, xc_s.at[w, slot(o)], xc_r.at[w, slot(o)], across_c)

    def span(q):
        return pl.ds(STARTS[q], SIZES[q])

    def stage_a(q):
        w, offsets = CHUNKS[q]
        for o in offsets:
            arrived(x_all.at[w, z_at(o), other_c], xc_s.at[w, slot(o)], xc_r.at[w, slot(o)], across_c)
        use(1)
        use(2)
        rows = jnp.concatenate([x_all[w, z_at(o)].reshape(64, 512) for o in offsets], axis=0)
        part_rows = span(q)
        for weight, dst in ((gate_v, gate_p), (up_v, up_p)):
            value = jnp.dot(rows, weight[...], preferred_element_type=F32).astype(BF)
            dst[:, part_rows] = value.reshape(NX, SIZES[q], 512)
        send(gate_p.at[xo, part_rows], m1g.at[part_rows], xp_s.at[q, 0], xp_r.at[q, 0], right)
        send(up_p.at[xo, part_rows], m1u.at[part_rows], xp_s.at[q, 1], xp_r.at[q, 1], left)
        send(up_p.at[xr, part_rows], m2u.at[part_rows], xp_s.at[q, 2], xp_r.at[q, 2], right)
        send(gate_p.at[xl, part_rows], m2g.at[part_rows], xp_s.at[q, 3], xp_r.at[q, 3], left)

    def stage_b(q):
        t = span(q)
        arrived(m1g.at[t], xp_s.at[q, 0], xp_r.at[q, 0], left)
        s3g[t] = (gate_p[xr, t].astype(F32) + m1g[t].astype(F32)).astype(BF)
        send(s3g.at[t], m3g.at[t], xp_s.at[q, 4], xp_r.at[q, 4], right)
        arrived(m1u.at[t], xp_s.at[q, 1], xp_r.at[q, 1], right)
        s3u[t] = (up_p[xl, t].astype(F32) + m1u[t].astype(F32)).astype(BF)
        send(s3u.at[t], m3u.at[t], xp_s.at[q, 5], xp_r.at[q, 5], left)

    def stage_c(q):
        t = span(q)
        arrived(m2u.at[t], xp_s.at[q, 2], xp_r.at[q, 2], left)
        arrived(m2g.at[t], xp_s.at[q, 3], xp_r.at[q, 3], right)
        arrived(m3g.at[t], xp_s.at[q, 4], xp_r.at[q, 4], left)
        arrived(m3u.at[t], xp_s.at[q, 5], xp_r.at[q, 5], right)
        gate = gate_p[x, t].astype(F32) + m2g[t].astype(F32) + m3g[t].astype(F32)
        up = up_p[x, t].astype(F32) + m2u[t].astype(F32) + m3u[t].astype(F32)
        gate, up = gate.astype(BF), up.astype(BF)
        for b in range(NH):
            columns = slice(b * HD, (b + 1) * HD)
            h_send[b, t] = jnp.concatenate([gate[:, columns], up[:, columns]], axis=1)
        for o in (2, 1, 3):
            place = lax.rem(h + o, NH)
            send(
                h_send.at[place, t], h_recv.at[o - 1, t],
                hp_s.at[q, o - 1], hp_r.at[q, o - 1], at_h(place),
            )

    def stage_d(q):
        t = span(q)
        for o in range(1, NH):
            arrived(
                h_recv.at[o - 1, t], hp_s.at[q, o - 1], hp_r.at[q, o - 1],
                at_h(lax.rem(h + NH - o, NH)),
            )
        total = h_send[h, t].astype(F32)
        for o in range(NH - 1):
            total = total + h_recv[o, t].astype(F32)
        gate, up = total[:, :HD], total[:, HD:]
        hid[x, h, t] = (gate / (1.0 + jnp.exp(-gate)) * up).astype(BF)
        block = hid.at[x, h, t]
        for o in (2, 1, 3):
            send(
                block, block, hg_s.at[q, o - 1], hg_r.at[q, o - 1], at_h(lax.rem(h + o, NH))
            )

    def stage_e(q):
        t = span(q)
        for o in range(1, NH):
            place = lax.rem(h + NH - o, NH)
            arrived(hid.at[x, place, t], hg_s.at[q, o - 1], hg_r.at[q, o - 1], at_h(place))
        block = hid.at[x, pl.ds(0, NH), t]
        send(block, block, xg_s.at[q, 0], xg_r.at[q, 0], right)
        send(block, block, xg_s.at[q, 1], xg_r.at[q, 1], left)

    def stage_f(q):
        t = span(q)
        arrived(hid.at[xl, pl.ds(0, NH), t], xg_s.at[q, 0], xg_r.at[q, 0], left)
        half = hid.at[xl, pl.ds(0, 2), t]
        send(half, half, xg_s.at[q, 2], xg_r.at[q, 2], right)
        arrived(hid.at[xr, pl.ds(0, NH), t], xg_s.at[q, 1], xg_r.at[q, 1], right)
        half = hid.at[xr, pl.ds(2, 2), t]
        send(half, half, xg_s.at[q, 3], xg_r.at[q, 3], left)

    def stage_g(q):
        t = span(q)
        arrived(hid.at[xo, pl.ds(0, 2), t], xg_s.at[q, 2], xg_r.at[q, 2], left)
        arrived(hid.at[xo, pl.ds(2, 2), t], xg_s.at[q, 3], xg_r.at[q, 3], right)
        use(3)
        rows = jnp.concatenate(
            [jnp.concatenate([hid[a, b, t] for b in range(NH)], axis=1) for a in range(NX)], axis=0
        )
        value = jnp.dot(rows, down_v[...], preferred_element_type=F32).astype(BF)
        count, first_block = SIZES[q] // 16, STARTS[q] // 16
        value = value.reshape(count, 2, 2, 16, 512)
        for b in range(count):
            part[:, first_block + b] = value[b]
        blocks = pl.ds(first_block, count)
        send(part.at[other_c, blocks], part_in.at[blocks], oc_s.at[q], oc_r.at[q], across_c)

    def stage_h(q):
        w, offsets = CHUNKS[q]
        first_block = STARTS[q] // 16
        blocks = pl.ds(first_block, SIZES[q] // 16)
        arrived(part_in.at[blocks], oc_s.at[q], oc_r.at[q], across_c)
        z_send[blocks] = (part[c, blocks].astype(F32) + part_in[blocks].astype(F32)).astype(BF)
        for b, o in enumerate(offsets):
            if o:
                send(
                    z_send.at[first_block + b], z_recv.at[w, slot(o)],
                    oz_s.at[w, slot(o)], oz_r.at[w, slot(o)], at_tp(z_at(o), l, c),
                )

    def start_l(w):
        offsets = []
        for q, (kind, places) in enumerate(CHUNKS):
            for b, o in enumerate(places):
                if kind == w and o:
                    offsets.append(o)
                elif kind == w:
                    total = z_send[STARTS[q] // 16 + b].astype(F32)
        for o in offsets:
            arrived(
                z_recv.at[w, slot(o)], oz_s.at[w, slot(o)], oz_r.at[w, slot(o)],
                at_tp(z_at(-o), l, c),
            )
            total = total + z_recv[w, slot(o)].astype(F32)
        l_send[w] = total.astype(BF)
        send(l_send.at[w, other_l], l_recv.at[w], ol_s.at[w], ol_r.at[w], across_l)

    def start_m(w):
        arrived(l_recv.at[w], ol_s.at[w], ol_r.at[w], across_l)
        ffn = l_send[w, l].astype(F32) + l_recv[w].astype(F32)
        for i in range(4):
            rows_out[w, pl.ds(i, DP, stride=4), :] = ffn[:, i * HD : (i + 1) * HD]
        if w == 0:
            for rank in range(DP):
                e_send[0, rank] = rows_out[0, 4 * rank : 4 * rank + 4]
        else:
            for rank in range(DP):
                fin[rank] = rows_out[1, 4 * rank : 4 * rank + 4] + in_listed[rank, 4:]
            for rank in range(DP):
                anchor = jnp.int32(rank)
                for i in range(MIG):
                    anchor = jnp.where(targets[i] == rank, sources[i], anchor)
                e_send[1, rank] = fin[anchor]
        exchange(e_send.at[w], e_recv.at[w], e_s.at[w], e_r.at[w])

    steps = {
        "local": local, "route": route, "listed": listed, "x": start_x, "y": start_y,
        "w": forward, "a": stage_a, "b": stage_b, "c": stage_c, "d": stage_d, "e": stage_e,
        "f": stage_f, "g": stage_g, "h": stage_h, "l": start_l, "m": start_m,
    }
    for step in ORDER:
        name = step.rstrip("0123456789")
        steps[name](int(step[len(name) :] or 0))

    all_left(c_local, c_s.at[0], c_r.at[0])
    all_left(c_listed, c_s.at[1], c_r.at[1])
    for copy in sent:
        copy.wait_send()
    for w in range(2):
        exchanged(e_recv.at[w], e_s.at[w], e_r.at[w])
        for k in range(DP):
            tiles[64 * w + 4 * k : 64 * w + 4 * k + 4] = e_recv[w, k]
    tiles[:64] = tiles[:64] + stream_local[...]
    value = jnp.concatenate([tiles[pl.ds(j, 2, stride=64), :] for j in range(64)], axis=1)
    out[...] = ordered(value).astype(BF)
    for w in range(2):
        all_left(e_send.at[w], e_s.at[w], e_r.at[w])


def on_device(
    queries, residual, new_entries, page_pool, page_table, cache_lengths, migration,
    norm_gain, gate_weight, up_weight, down_weight,
):
    pages, page_rows, entry = page_pool.shape[2:]
    vmem = pl.BlockSpec(memory_space=pltpu.VMEM)
    hbm = pl.BlockSpec(memory_space=pl.ANY)
    smem = pl.BlockSpec(memory_space=pltpu.SMEM)
    nq = len(CHUNKS)
    dma = pltpu.SemaphoreType.DMA
    share = (256, 512)
    scratch = [
        pltpu.VMEM((512, 2048), BF),
        pltpu.VMEM((512, 512), BF), pltpu.VMEM((512, 512), BF), pltpu.VMEM((512, 512), BF),
        pltpu.VMEM((128, HD), F32), pltpu.VMEM((128, HD), F32), pltpu.VMEM((32, HD), F32),
        pltpu.VMEM((144, HD), BF), pltpu.VMEM((NX, 144, HD), BF),
        pltpu.VMEM((NH - 1, 144, HD), BF), pltpu.VMEM((NH, 144, HD), BF),
        pltpu.VMEM((DP, 4, HD), F32), pltpu.VMEM((DP, 8, HD), F32),
        pltpu.VMEM((DP, 4, HD), F32), pltpu.VMEM((DP, 8, HD), F32),
        pltpu.VMEM((64, HD), F32), pltpu.VMEM((DP * 8, HD), F32),
        pltpu.VMEM((2, NZ, 2, 2, 16, 512), BF),
        pltpu.VMEM((NX,) + share, BF), pltpu.VMEM((NX,) + share, BF),
    ]
    scratch += [pltpu.VMEM(share, BF) for _ in range(8)]
    scratch += [
        pltpu.VMEM((NH, 256, 256), BF), pltpu.VMEM((NH - 1, 256, 256), BF),
        pltpu.VMEM((NX, NH, 256, HD), BF),
        pltpu.VMEM((2, 16, 2, 16, 512), BF), pltpu.VMEM((16, 2, 16, 512), BF),
        pltpu.VMEM((16, 2, 16, 512), BF), pltpu.VMEM((2, NZ, 2, 16, 512), BF),
        pltpu.VMEM((2, 2, 16, 512), BF), pltpu.VMEM((2, 16, 512), BF),
        pltpu.VMEM((2, 64, HD), F32), pltpu.VMEM((DP, 4, HD), F32),
        pltpu.VMEM((2, DP, 4, HD), F32), pltpu.VMEM((2, DP, 4, HD), F32),
    ]
    scratch += [dma((4,))]
    scratch += [dma((3,)) for _ in range(4)]
    scratch += [dma((2,)), dma((2,)), dma((2,)), dma((2,))]
    scratch += [dma((2,)), dma((2,)), dma((2, NZ)), dma((2, NZ)), dma((2, NZ)), dma((2, NZ))]
    scratch += [dma((nq, 6)), dma((nq, 6)), dma((nq, 3)), dma((nq, 3)), dma((nq, 3)), dma((nq, 3))]
    scratch += [dma((nq, 4)), dma((nq, 4)), dma((nq,)), dma((nq,)), dma((2, NZ)), dma((2, NZ))]
    scratch += [dma((2,)), dma((2,))]
    done = pl.pallas_call(
        kernel,
        out_shape=jax.ShapeDtypeStruct((2, DP * 4 * HD), BF),
        in_specs=[smem, smem, smem, vmem, vmem, vmem, vmem, hbm, hbm, hbm, hbm],
        out_specs=vmem,
        scratch_shapes=scratch,
        compiler_params=pltpu.CompilerParams(
            collective_id=0, has_side_effects=True, vmem_limit_bytes=62 * 1024 * 1024
        ),
    )(
        migration.transpose(1, 0, 2), page_table[0, 0], cache_lengths[0, 0],
        queries[0, 0], residual[0, 0], new_entries[0, 0], norm_gain.reshape(DP * 4, HD),
        page_pool.reshape(pages * page_rows, entry), gate_weight, up_weight, down_weight,
    )
    return done.reshape(1, 1, 2, DP * 4 * HD)


def solution(mesh):
    return jax.shard_map(
        on_device,
        mesh=mesh,
        in_specs=(
            P("dp", "tp", None, None),
            P("dp", "tp", None, None),
            P("dp", "tp", None, None),
            P("dp", "tp", None, None, None),
            P("dp", "tp", None, None),
            P("dp", "tp", None),
            P("tp", None, None),
            P(),
            P("dp", "tp"),
            P("dp", "tp"),
            P("tp", "dp"),
        ),
        out_specs=P("dp", "tp", None, None),
        check_vma=False,
    )
```

```python
import math

import jax
import jax.numpy as jnp
from jax import lax
from jax.experimental import pallas as pl
from jax.experimental.pallas import tpu as pltpu
from jax.sharding import PartitionSpec as P

HD = 128
KVH = 8
NX, NH, NZ = 4, 4, 8
DP = NX * NH
MIG = 3
MAXP, PG = 16, 16
PLACES = (0, 1, -1, 2, -2, 3, -3, 4)
CHUNKS = (
    (0, (0, 1)), (0, (-1, 2, -2, 3)), (0, (-3, 4)), (1, (-3, 4)), (1, (-1, 2, -2, 3)),
    (1, (0, 1)),
)
SIZES = [8 * len(offsets) for _, offsets in CHUNKS]
STARTS = [sum(SIZES[:q]) for q in range(len(CHUNKS))]
ORDER = (
    "local", "x0", "route", "y0", "r01", "listed", "r02", "a0", "x1", "r03", "c0", "y1", "a1",
    "r04", "r11", "d0", "a2", "r12", "c1", "a5", "r13", "c2", "e0", "a4", "r14", "c5", "d2", "d1",
    "a3", "c4", "e2", "f0", "e1", "d5", "c3", "f2", "g0", "f1", "d4", "g2", "d3", "e5", "h0",
    "e4", "h2", "e3", "g1", "f3", "f4", "f5", "h1", "g3", "g4", "h3", "g5", "h4", "l0", "h5",
    "m0", "l1", "m1",
)
DISTANCES = (10, 9, 11, 8, 6, 14, 2, 5, 7, 13, 15, 4, 12, 1, 3)
EPSILON = 1e-05
BF = jnp.bfloat16
F32 = jnp.float32


def kernel(
    mig, table, lengths, q_in, res_in, new_in, gain, pool, gate_w, up_w, down_w, out,
    pool_v, weight, down_v,
    q_t, res_t, new_t, own, line, y_send, y_recv, c_local, c_listed, in_local, in_listed,
    stream_local, tiles, x_all,
    sums, sums_in, h_send, h_recv, hid, part, part_in, z_send, z_recv, l_send, l_recv,
    rows_out, fin, e_send, e_recv,
    load_sem, rx_s, rx_r, ry_s, ry_r, c_s, c_r, e_s, e_r,
    w_s, w_r, xl_s, xl_r, xz_s, xz_r, xc_s, xc_r,
    xp_s, xp_r, hp_s, hp_r, hg_s, hg_r, xg_s, xg_r,
    oc_s, oc_r, oz_s, oz_r, ol_s, ol_r,
):
    dp, tp = lax.axis_index("dp"), lax.axis_index("tp")
    h, x = lax.div(dp, NX), lax.rem(dp, NX)
    z, low = lax.div(tp, 4), lax.rem(tp, 4)
    l, c = lax.div(low, 2), lax.rem(low, 2)
    other_l, other_c = 1 - l, 1 - c
    parity, side = lax.rem(x, 2), lax.div(x, 2)
    half = lax.rem(lax.div(x + 1, 2), 2)
    mate, like = x + 1 - 2 * parity, NX - 1 - x
    other_side, opposite = 1 - side, NX - 1 - mate
    at_mate, at_like = (h * NX + mate, tp), (h * NX + like, tp)

    def at_dp(rank):
        return (rank, tp)

    def at_h(place):
        return (place * NX + x, tp)

    def at_tp(zz, ll, cc):
        return (dp, zz * 4 + ll * 2 + cc)

    def z_at(offset):
        return lax.rem(z + (offset + NZ), NZ)

    def slot(offset):
        return (offset + NZ) % NZ

    across_l, across_c = at_tp(z, other_l, c), at_tp(z, l, other_c)
    sent = []

    def send(src, dst, send_sem, recv_sem, device, listed_copy=True):
        copy = pltpu.make_async_remote_copy(
            src_ref=src, dst_ref=dst, send_sem=send_sem, recv_sem=recv_sem,
            device_id=device, device_id_type=pl.DeviceIdType.MESH,
        )
        copy.start()
        if listed_copy:
            sent.append(copy)

    def arrived(dst, send_sem, recv_sem, device):
        pltpu.make_async_remote_copy(
            src_ref=dst, dst_ref=dst, send_sem=send_sem, recv_sem=recv_sem,
            device_id=device, device_id_type=pl.DeviceIdType.MESH,
        ).wait_recv()

    def columns_of(array, which):
        return array.at[:, pl.ds(pl.multiple_of(which * 256, 256), 256)]

    loads = [
        pltpu.make_async_copy(src, dst, load_sem.at[i])
        for i, (src, dst) in enumerate(
            (
                (pool, pool_v),
                (columns_of(gate_w, half), weight.at[parity, :, pl.ds(0, 256)]),
                (columns_of(up_w, half), weight.at[parity, :, pl.ds(256, 256)]),
                (down_w, down_v),
            )
        )
    ]
    for copy in loads:
        copy.start()
    waiting = set(range(len(loads) + 1))

    def use(i):
        if i in waiting:
            waiting.discard(i)
            loads[i].wait()


    others = [lax.rem(h + o // NX, NH) * NX + lax.rem(x + o % NX, NX) for o in DISTANCES]
    barrier = pltpu.get_barrier_semaphore()
    partners = [at_dp(rank) for rank in others]
    partners += [at_tp(z_at(o), l, c) for o in range(1, NZ)] + [across_l, across_c]
    for device in partners:
        pl.semaphore_signal(barrier, inc=1, device_id=device, device_id_type=pl.DeviceIdType.MESH)

    def exchange(src, dst, s_sem, r_sem, share=1):
        for rank in others:
            part = src.at[lax.div(rank, share)] if share > 1 else src.at[rank]
            send(part, dst.at[dp], s_sem, r_sem, at_dp(rank), False)
        dst[dp] = src[lax.div(dp, share)] if share > 1 else src[dp]

    def exchanged(dst, s_sem, r_sem):
        arrived(dst.at[pl.ds(0, DP - 1)], s_sem, r_sem, at_dp(others[0]))

    def all_left(src, s_sem, r_sem):
        part = src.at[pl.ds(0, DP - 1)]
        pltpu.make_async_remote_copy(
            src_ref=part, dst_ref=part, send_sem=s_sem, recv_sem=r_sem,
            device_id=at_dp(others[0]), device_id_type=pl.DeviceIdType.MESH,
        ).wait_send()

    slot_id = mig[0, 0, 0]
    second = slot_id == 1

    def ordered(value):
        return jnp.where(second, value, jnp.concatenate([value[1:2], value[0:1]], axis=0))

    for source, dst, count in ((q_in, q_t, 64), (res_in, res_t, 64), (new_in, new_t, 16)):
        value = ordered(source[...].astype(F32))
        for j in range(count):
            dst[pl.ds(j, 2, stride=count), :] = value[:, j * HD : (j + 1) * HD]

    own[...] = jnp.concatenate([q_t[64:], res_t[64:], new_t[16:]], axis=0).astype(BF)

    def bias_of(place):
        lane = lax.broadcasted_iota(jnp.int32, (8, MAXP * 2 * PG), 1)
        page, inner = lane // PG, lane % PG
        length = lengths[place]
        filled = jnp.zeros_like(lane)
        for p in range(MAXP):
            held = jnp.minimum(jnp.maximum(length - p * PG, 0), PG)
            filled = jnp.where(page == table[place, p], held, filled)
        return jnp.where(inner < filled, 0.0, -1e30)

    def attend(q_rows, res_rows, new_rows, hidden_bias):
        factor = 1.0 / math.sqrt(HD)
        new_keys = jnp.stack([new_rows[j : j + 1] for j in range(KVH)])
        new_values = jnp.stack([new_rows[KVH + j : KVH + j + 1] for j in range(KVH)])
        q_bf = q_rows.astype(BF)
        score = jnp.stack(
            [
                lax.dot_general(
                    q_bf[head], pool_v[:, head * HD : (head + 1) * HD],
                    (((1,), (1,)), ((), ())), preferred_element_type=F32,
                )
                for head in range(KVH)
            ]
        )
        score = score * factor + hidden_bias[None]
        own_score = jnp.sum(q_rows * new_keys, axis=-1, keepdims=True) * factor
        top = jnp.maximum(jnp.max(score, axis=-1, keepdims=True), own_score)
        exponent = jnp.exp(score - top)
        own_exponent = jnp.exp(own_score - top)
        scale = 1.0 / (jnp.sum(exponent, axis=-1, keepdims=True) + own_exponent)
        weight = (exponent * scale).astype(BF)
        own_weight = (own_exponent * scale).astype(BF).astype(F32)
        attended = jnp.stack(
            [
                jnp.dot(
                    weight[head], pool_v[:, (KVH + head) * HD : (KVH + head + 1) * HD],
                    preferred_element_type=F32,
                )
                for head in range(KVH)
            ]
        )
        stream = res_rows + attended + own_weight * new_values
        square = jnp.sum(jnp.sum(stream * stream, axis=0), axis=-1, keepdims=True)
        mean = jnp.sum(square, axis=0, keepdims=True) * (1.0 / (DP * 4 * HD))
        scale = lax.rsqrt(mean + EPSILON)
        normed = stream * scale[None] * gain[...].astype(F32).reshape(KVH, 8, HD)
        return normed, stream

    def local(_):
        local_q = q_t[:64].reshape(KVH, 8, HD)
        local_res = res_t[:64].reshape(KVH, 8, HD)
        hidden_bias = bias_of(1 - slot_id)
        use(0)
        normed, stream = attend(local_q, local_res, new_t[:16], hidden_bias)
        stream_local[...] = stream.reshape(DP * 4, HD)
        c_local[...] = normed
        pl.semaphore_wait(barrier, len(partners))
        exchange(c_local, in_local, c_s.at[0], c_r.at[0], 2)
        for o in range(1, NX):
            send(
                own, line.at[x], rx_s.at[o - 1], rx_r.at[o - 1],
                (h * NX + lax.rem(x + o, NX), tp),
            )
        line[x] = own[...]
        for i, array in enumerate((gate_w, up_w)):
            dst = weight.at[parity, :, pl.ds(256 * i, 256)]
            send(columns_of(array, 1 - half), dst, w_s.at[i], w_r.at[i], at_mate)

    sources = [mig[i, 0, 1] for i in range(MIG)]
    targets = [mig[i, 0, 2] for i in range(MIG)]

    def route(_):
        for o in range(1, NX):
            place = lax.rem(x + NX - o, NX)
            arrived(line.at[place], rx_s.at[o - 1], rx_r.at[o - 1], (h * NX + place, tp))
        rows = [line[lax.rem(target, NX)].astype(F32) for target in targets]
        here = [lax.div(target, NX) == h for target in targets]

        def wanted(rank):
            value = jnp.zeros_like(rows[0])
            for i in range(MIG):
                value = jnp.where(here[i] & (sources[i] == rank), rows[i], value)
            return value.astype(BF)

        for o in range(1, NH):
            place = lax.rem(h + o, NH)
            y_send[o - 1] = wanted(place * NX + x)
            send(
                y_send.at[o - 1], y_recv.at[o - 1], ry_s.at[o - 1], ry_r.at[o - 1], at_h(place)
            )
        y_recv[NH - 1] = wanted(dp)

    def listed(_):
        for o in range(1, NH):
            arrived(
                y_recv.at[o - 1], ry_s.at[o - 1], ry_r.at[o - 1], at_h(lax.rem(h + NH - o, NH))
            )
        routed = y_recv[NH - 1].astype(F32)
        for o in range(NH - 1):
            routed = routed + y_recv[o].astype(F32)
        serves = (sources[0] == dp) | (sources[1] == dp) | (sources[2] == dp)
        row = jnp.where(serves, routed, own[...].astype(F32))
        normed, stream = attend(
            row[:64].reshape(KVH, 8, HD), row[64:128].reshape(KVH, 8, HD), row[128:],
            bias_of(slot_id),
        )
        c_listed[...] = jnp.concatenate([normed, stream], axis=1).astype(BF)
        exchange(c_listed, in_listed, c_s.at[1], c_r.at[1], 2)

    def start_x(w):
        source = in_local if w == 0 else in_listed
        exchanged(source, c_s.at[w], c_r.at[w])
        rows = source[...] if w == 0 else source[:, :8].astype(F32)
        tiles[...] = rows.reshape(DP * 8, HD)
        x_all[w, 0, c, l] = jnp.concatenate(
            [tiles[pl.ds(i, DP, stride=8), :] for i in range(8)], axis=1
        ).astype(BF)
        block = x_all.at[w, 0, c, l]
        send(block, block, xl_s.at[w], xl_r.at[w], across_l)

    def place_of(w, o):
        return x_all.at[w, PLACES.index(o), c]

    def pass_on(w, o):
        for step, device in ((1, at_tp(z_at(-1), l, c)), (-1, at_tp(z_at(1), l, c))):
            to = o + step
            if (o == 0 or o * step > 0) and to in PLACES:
                send(
                    place_of(w, o), place_of(w, to),
                    xz_s.at[w, slot(to)], xz_r.at[w, slot(to)], device,
                )

    def start_y(w):
        arrived(x_all.at[w, 0, c, other_l], xl_s.at[w], xl_r.at[w], across_l)
        pass_on(w, 0)

    def ring(code):
        w, i = code // 10, code % 10
        for o in (i, -i):
            if o in PLACES:
                source = at_tp(z_at(1 if o > 0 else -1), l, c)
                arrived(place_of(w, o), xz_s.at[w, slot(o)], xz_r.at[w, slot(o)], source)
                pass_on(w, o)
        blocks = x_all.at[w, pl.ds(2 * i - 2, 2), c]
        send(blocks, blocks, xc_s.at[w, i - 1], xc_r.at[w, i - 1], across_c)

    def span(q, count=1):
        return pl.ds(STARTS[q] * count, SIZES[q] * count)

    def stage_a(q):
        w, offsets = CHUNKS[q]
        first, count = PLACES.index(offsets[0]), len(offsets)
        for i in range(first // 2, (first + count) // 2):
            blocks = x_all.at[w, pl.ds(2 * i, 2), other_c]
            arrived(blocks, xc_s.at[w, i], xc_r.at[w, i], across_c)
        use(1)
        use(2)
        if 4 in waiting:
            waiting.discard(4)
            for i in range(2):
                dst = weight.at[1 - parity, :, pl.ds(256 * i, 256)]
                arrived(dst, w_s.at[i], w_r.at[i], at_mate)
        rows = x_all[w, first : first + count].reshape(64 * count, 1024)
        value = jnp.dot(
            rows, weight[...].reshape(1024, 512), preferred_element_type=F32
        ).astype(BF)
        t = span(q, 4)
        sums[:, t] = value.reshape(2, 4 * SIZES[q], 512)
        send(sums.at[other_side, t], sums_in.at[t], xp_s.at[q], xp_r.at[q], at_like)

    def stage_c(q):
        t = span(q, 4)
        arrived(sums_in.at[t], xp_s.at[q], xp_r.at[q], at_like)
        value = (sums[side, t].astype(F32) + sums_in[t].astype(F32)).astype(BF)
        t = span(q)
        h_send[:, t] = value.reshape(NH, SIZES[q], 512)
        for o in (2, 1, 3):
            place = lax.rem(h + o, NH)
            send(
                h_send.at[place, t], h_recv.at[o - 1, t],
                hp_s.at[q, o - 1], hp_r.at[q, o - 1], at_h(place),
            )

    def stage_d(q):
        t = span(q)
        for o in range(1, NH):
            arrived(
                h_recv.at[o - 1, t], hp_s.at[q, o - 1], hp_r.at[q, o - 1],
                at_h(lax.rem(h + NH - o, NH)),
            )
        total = h_send[h, t].astype(F32)
        for o in range(NH - 1):
            total = total + h_recv[o, t].astype(F32)
        gate, up = total[:, :256], total[:, 256:]
        hid[x, h, t] = (gate / (1.0 + jnp.exp(-gate)) * up).astype(BF)
        block = hid.at[x, h, t]
        for o in (2, 1, 3):
            send(
                block, block, hg_s.at[q, o - 1], hg_r.at[q, o - 1], at_h(lax.rem(h + o, NH))
            )

    def stage_e(q):
        t = span(q)
        for o in range(1, NH):
            place = lax.rem(h + NH - o, NH)
            arrived(hid.at[x, place, t], hg_s.at[q, o - 1], hg_r.at[q, o - 1], at_h(place))
        block = hid.at[x, pl.ds(0, NH), t]
        send(block, block, xg_s.at[q, 0], xg_r.at[q, 0], at_like)
        send(block, block, xg_s.at[q, 1], xg_r.at[q, 1], at_mate)

    def stage_f(q):
        block = hid.at[like, pl.ds(0, NH), span(q)]
        arrived(block, xg_s.at[q, 0], xg_r.at[q, 0], at_like)
        send(block, block, xg_s.at[q, 2], xg_r.at[q, 2], at_mate)

    def stage_g(q):
        t = span(q)
        for i, place in ((1, mate), (2, opposite)):
            arrived(hid.at[place, pl.ds(0, NH), t], xg_s.at[q, i], xg_r.at[q, i], at_mate)
        use(3)
        rows = jnp.concatenate(
            [
                jnp.concatenate([hid[first, b, t], hid[second_half, b, t]], axis=1)
                for first, second_half in ((0, 1), (3, 2))
                for b in range(NH)
            ],
            axis=0,
        )
        value = jnp.dot(rows, down_v[...], preferred_element_type=F32).astype(BF)
        count, first_block = SIZES[q] // 8, STARTS[q] // 8
        value = value.reshape(count, 2, 2, 16, 512)
        for b in range(count):
            part[:, first_block + b] = value[b]
        blocks = pl.ds(first_block, count)
        send(part.at[other_c, blocks], part_in.at[blocks], oc_s.at[q], oc_r.at[q], across_c)

    def stage_h(q):
        w, offsets = CHUNKS[q]
        first_block = STARTS[q] // 8
        blocks = pl.ds(first_block, SIZES[q] // 8)
        arrived(part_in.at[blocks], oc_s.at[q], oc_r.at[q], across_c)
        z_send[blocks] = (part[c, blocks].astype(F32) + part_in[blocks].astype(F32)).astype(BF)
        for b, o in enumerate(offsets):
            if o:
                send(
                    z_send.at[first_block + b], z_recv.at[w, slot(o)],
                    oz_s.at[w, slot(o)], oz_r.at[w, slot(o)], at_tp(z_at(o), l, c),
                )

    def start_l(w):
        offsets = []
        for q, (kind, places) in enumerate(CHUNKS):
            for b, o in enumerate(places):
                if kind == w and o:
                    offsets.append(o)
                elif kind == w:
                    total = z_send[STARTS[q] // 8 + b].astype(F32)
        for o in offsets:
            arrived(
                z_recv.at[w, slot(o)], oz_s.at[w, slot(o)], oz_r.at[w, slot(o)],
                at_tp(z_at(-o), l, c),
            )
            total = total + z_recv[w, slot(o)].astype(F32)
        l_send[w] = total.astype(BF)
        send(l_send.at[w, other_l], l_recv.at[w], ol_s.at[w], ol_r.at[w], across_l)

    def start_m(w):
        arrived(l_recv.at[w], ol_s.at[w], ol_r.at[w], across_l)
        ffn = l_send[w, l].astype(F32) + l_recv[w].astype(F32)
        for i in range(4):
            rows_out[w, pl.ds(i, DP, stride=4), :] = ffn[:, i * HD : (i + 1) * HD]
        if w == 0:
            for rank in range(DP):
                e_send[0, rank] = rows_out[0, 4 * rank : 4 * rank + 4]
        else:
            for rank in range(DP):
                stream = in_listed[rank, 8:].astype(F32)
                stream = jnp.where(parity == 1, stream[4:], stream[:4])
                fin[rank] = rows_out[1, 4 * rank : 4 * rank + 4] + stream
            for rank in range(DP):
                anchor = jnp.int32(rank)
                for i in range(MIG):
                    anchor = jnp.where(targets[i] == rank, sources[i], anchor)
                e_send[1, rank] = fin[anchor]
        exchange(e_send.at[w], e_recv.at[w], e_s.at[w], e_r.at[w])

    steps = {
        "local": local, "route": route, "listed": listed, "x": start_x, "y": start_y,
        "r": ring, "a": stage_a, "c": stage_c, "d": stage_d, "e": stage_e,
        "f": stage_f, "g": stage_g, "h": stage_h, "l": start_l, "m": start_m,
    }
    for step in ORDER:
        name = step.rstrip("0123456789")
        steps[name](int(step[len(name) :] or 0))

    all_left(in_local, c_s.at[0], c_r.at[0])
    all_left(in_listed, c_s.at[1], c_r.at[1])
    for copy in sent:
        copy.wait_send()
    for w in range(2):
        exchanged(e_recv.at[w], e_s.at[w], e_r.at[w])
        for k in range(DP):
            tiles[64 * w + 4 * k : 64 * w + 4 * k + 4] = e_recv[w, k]
    tiles[:64] = tiles[:64] + stream_local[...]
    value = jnp.concatenate([tiles[pl.ds(j, 2, stride=64), :] for j in range(64)], axis=1)
    out[...] = ordered(value).astype(BF)
    for w in range(2):
        all_left(e_send.at[w], e_s.at[w], e_r.at[w])


def on_device(
    queries, residual, new_entries, page_pool, page_table, cache_lengths, migration,
    norm_gain, gate_weight, up_weight, down_weight,
):
    pages, page_rows, entry = page_pool.shape[2:]
    vmem = pl.BlockSpec(memory_space=pltpu.VMEM)
    hbm = pl.BlockSpec(memory_space=pl.ANY)
    smem = pl.BlockSpec(memory_space=pltpu.SMEM)
    nq = len(CHUNKS)
    dma = pltpu.SemaphoreType.DMA
    scratch = [
        pltpu.VMEM((512, 2048), BF),
        pltpu.VMEM((2, 512, 512), BF), pltpu.VMEM((512, 512), BF),
        pltpu.VMEM((128, HD), F32), pltpu.VMEM((128, HD), F32), pltpu.VMEM((32, HD), F32),
        pltpu.VMEM((144, HD), BF), pltpu.VMEM((NX, 144, HD), BF),
        pltpu.VMEM((NH - 1, 144, HD), BF), pltpu.VMEM((NH, 144, HD), BF),
        pltpu.VMEM((KVH, 8, HD), F32), pltpu.VMEM((KVH, 16, HD), BF),
        pltpu.VMEM((DP, 8, HD), F32), pltpu.VMEM((DP, 16, HD), BF),
        pltpu.VMEM((64, HD), F32), pltpu.VMEM((DP * 8, HD), F32),
        pltpu.VMEM((2, NZ, 2, 2, 16, 1024), BF),
        pltpu.VMEM((2, 512, 512), BF), pltpu.VMEM((512, 512), BF),
        pltpu.VMEM((NH, 128, 512), BF), pltpu.VMEM((NH - 1, 128, 512), BF),
        pltpu.VMEM((NX, NH, 128, 256), BF),
        pltpu.VMEM((2, 16, 2, 16, 512), BF), pltpu.VMEM((16, 2, 16, 512), BF),
        pltpu.VMEM((16, 2, 16, 512), BF), pltpu.VMEM((2, NZ, 2, 16, 512), BF),
        pltpu.VMEM((2, 2, 16, 512), BF), pltpu.VMEM((2, 16, 512), BF),
        pltpu.VMEM((2, 64, HD), F32), pltpu.VMEM((DP, 4, HD), F32),
        pltpu.VMEM((2, DP, 4, HD), F32), pltpu.VMEM((2, DP, 4, HD), F32),
    ]
    scratch += [dma((4,))]
    scratch += [dma((3,)) for _ in range(4)]
    scratch += [dma((2,)), dma((2,)), dma((2,)), dma((2,))]
    scratch += [dma((2,)), dma((2,))]
    scratch += [dma((2,)), dma((2,)), dma((2, NZ)), dma((2, NZ)), dma((2, 4)), dma((2, 4))]
    scratch += [dma((nq,)), dma((nq,)), dma((nq, 3)), dma((nq, 3)), dma((nq, 3)), dma((nq, 3))]
    scratch += [dma((nq, 3)), dma((nq, 3)), dma((nq,)), dma((nq,)), dma((2, NZ)), dma((2, NZ))]
    scratch += [dma((2,)), dma((2,))]
    done = pl.pallas_call(
        kernel,
        out_shape=jax.ShapeDtypeStruct((2, DP * 4 * HD), BF),
        in_specs=[smem, smem, smem, vmem, vmem, vmem, vmem, hbm, hbm, hbm, hbm],
        out_specs=vmem,
        scratch_shapes=scratch,
        compiler_params=pltpu.CompilerParams(
            collective_id=0, has_side_effects=True, vmem_limit_bytes=62 * 1024 * 1024
        ),
    )(
        migration.transpose(1, 0, 2), page_table[0, 0], cache_lengths[0, 0],
        queries[0, 0], residual[0, 0], new_entries[0, 0], norm_gain.reshape(DP * 4, HD),
        page_pool.reshape(pages * page_rows, entry), gate_weight, up_weight, down_weight,
    )
    return done.reshape(1, 1, 2, DP * 4 * HD)


def solution(mesh):
    return jax.shard_map(
        on_device,
        mesh=mesh,
        in_specs=(
            P("dp", "tp", None, None),
            P("dp", "tp", None, None),
            P("dp", "tp", None, None),
            P("dp", "tp", None, None, None),
            P("dp", "tp", None, None),
            P("dp", "tp", None),
            P("tp", None, None),
            P(),
            P("dp", "tp"),
            P("dp", "tp"),
            P("tp", "dp"),
        ),
        out_specs=P("dp", "tp", None, None),
        check_vma=False,
    )
```

```python
import math

import jax
import jax.numpy as jnp
from jax import lax
from jax.experimental import pallas as pl
from jax.experimental.pallas import tpu as pltpu
from jax.sharding import PartitionSpec as P

HD = 128
KVH = 8
NX, NH, NZ = 4, 4, 8
DP = NX * NH
MIG = 3
MAXP, PG = 16, 16
CHUNKS = (
    (0, (0, 1)), (0, (-1, 2)), (0, (-2, 3)), (0, (-3, 4)),
    (1, (-3, 4)), (1, (-2, 3)), (1, (-1, 2)), (1, (0, 1)),
)
SIZES = [16 * len(offsets) for _, offsets in CHUNKS]
STARTS = [sum(SIZES[:q]) for q in range(len(CHUNKS))]
ORDER = (
    "local", "x0", "route0", "route1", "y0", "listed0", "listed1", "w0", "listed2", "w2", "a0",
    "w1", "a2", "x1", "w3", "b0", "a1", "y1", "b1", "c0", "b2", "a3", "c1", "w4", "c2", "b3",
    "w5", "d0", "a4", "w6", "a5", "c3", "d2", "a6", "w7", "d1", "b5", "b4", "b6", "e0", "d3",
    "a7", "c5", "e2", "c4", "f0", "b7", "c6", "f2", "e1", "d5", "e3", "d4", "g2", "c7", "f1",
    "f3", "e5", "g0", "h2", "e4", "d6", "d7", "g3", "f4", "f5", "e6", "g1", "h3", "e7", "g4",
    "h0", "h1", "f6", "g5", "f7", "h4", "g6", "h5", "l0", "g7", "h6", "h7", "m0", "l1", "m1",
)
ROUTED = (pl.ds(0, 80), pl.ds(80, 64))
DISTANCES = (10, 9, 11, 8, 6, 14, 2, 5, 7, 13, 15, 4, 12, 1, 3)
EPSILON = 1e-05
BF = jnp.bfloat16
F32 = jnp.float32


def kernel(
    mig, table, lengths, q_in, res_in, new_in, gain, pool, gate_w, up_w, down_w, out,
    pool_v, gate_v, up_v, down_v,
    q_t, res_t, new_t, own, line_q, line_res, y_send, y_recv, c_local, c_listed, in_local, in_listed,
    stream_local, routed_row, attended_row, bias_row, tiles, x_all,
    gate_p, up_p, m1g, m1u, m2g, m2u, s3g, s3u, m3g, m3u,
    h_send, h_recv, hid, part, part_in, z_send, z_recv, l_send, l_recv,
    rows_out, fin, e_send, e_recv,
    load_sem, rx_s, rx_r, ry_s, ry_r, c_s, c_r, e_s, e_r,
    xl_s, xl_r, xz_s, xz_r, xc_s, xc_r,
    xp_s, xp_r, hp_s, hp_r, hg_s, hg_r, xg_s, xg_r,
    oc_s, oc_r, oz_s, oz_r, ol_s, ol_r,
):
    dp, tp = lax.axis_index("dp"), lax.axis_index("tp")
    h, x = lax.div(dp, NX), lax.rem(dp, NX)
    z, low = lax.div(tp, 4), lax.rem(tp, 4)
    l, c = lax.div(low, 2), lax.rem(low, 2)
    other_l, other_c = 1 - l, 1 - c
    xr, xo, xl = lax.rem(x + 1, NX), lax.rem(x + 2, NX), lax.rem(x + 3, NX)
    right, left = (h * NX + xr, tp), (h * NX + xl, tp)

    def at_dp(rank):
        return (rank, tp)

    def at_h(place):
        return (place * NX + x, tp)

    def at_tp(zz, ll, cc):
        return (dp, zz * 4 + ll * 2 + cc)

    def z_at(offset):
        return lax.rem(z + (offset + NZ), NZ)

    def slot(offset):
        return (offset + NZ) % NZ

    across_l, across_c = at_tp(z, other_l, c), at_tp(z, l, other_c)
    sent = []

    def send(src, dst, send_sem, recv_sem, device, listed_copy=True):
        copy = pltpu.make_async_remote_copy(
            src_ref=src, dst_ref=dst, send_sem=send_sem, recv_sem=recv_sem,
            device_id=device, device_id_type=pl.DeviceIdType.MESH,
        )
        copy.start()
        if listed_copy:
            sent.append(copy)

    def arrived(dst, send_sem, recv_sem, device):
        pltpu.make_async_remote_copy(
            src_ref=dst, dst_ref=dst, send_sem=send_sem, recv_sem=recv_sem,
            device_id=device, device_id_type=pl.DeviceIdType.MESH,
        ).wait_recv()

    loads = [
        pltpu.make_async_copy(src, dst, load_sem.at[i])
        for i, (src, dst) in enumerate(
            ((pool, pool_v), (gate_w, gate_v), (up_w, up_v), (down_w, down_v))
        )
    ]
    for copy in loads:
        copy.start()
    waiting = set(range(len(loads)))

    def use(i):
        if i in waiting:
            waiting.discard(i)
            loads[i].wait()


    others = [lax.rem(h + o // NX, NH) * NX + lax.rem(x + o % NX, NX) for o in DISTANCES]
    barrier = pltpu.get_barrier_semaphore()
    partners = [at_dp(rank) for rank in others]
    partners += [at_tp(z_at(o), l, c) for o in range(1, NZ)] + [across_l, across_c]
    for device in partners:
        pl.semaphore_signal(barrier, inc=1, device_id=device, device_id_type=pl.DeviceIdType.MESH)

    def exchange(src, dst, s_sem, r_sem):
        for rank in others:
            send(src.at[rank], dst.at[dp], s_sem, r_sem, at_dp(rank), False)
        dst[dp] = src[dp]

    def exchanged(dst, s_sem, r_sem):
        arrived(dst.at[pl.ds(0, DP - 1)], s_sem, r_sem, at_dp(others[0]))

    def all_left(src, s_sem, r_sem):
        part = src.at[pl.ds(0, DP - 1)]
        pltpu.make_async_remote_copy(
            src_ref=part, dst_ref=part, send_sem=s_sem, recv_sem=r_sem,
            device_id=at_dp(others[0]), device_id_type=pl.DeviceIdType.MESH,
        ).wait_send()

    slot_id = mig[0, 0, 0]
    second = slot_id == 1

    def ordered(value):
        return jnp.where(second, value, jnp.concatenate([value[1:2], value[0:1]], axis=0))

    for source, dst, count in ((q_in, q_t, 64), (res_in, res_t, 64), (new_in, new_t, 16)):
        value = ordered(source[...].astype(F32))
        for j in range(count):
            dst[pl.ds(j, 2, stride=count), :] = value[:, j * HD : (j + 1) * HD]

    top_half = lax.broadcasted_iota(jnp.int32, (KVH, 8, HD), 1) < 4

    def turned(value):
        return jnp.concatenate([value[:, 4:], value[:, :4]], axis=1)

    def pieces(first, second_value):
        even = jnp.where(top_half, first, turned(second_value))
        odd = jnp.where(top_half, turned(first), second_value)
        return even, odd

    own[...] = jnp.concatenate([q_t[64:], new_t[16:], res_t[64:]], axis=0).astype(BF)

    def bias_of(place):
        lane = lax.broadcasted_iota(jnp.int32, (8, MAXP * 2 * PG), 1)
        page, inner = lane >> 4, lane & 15
        length = lengths[place]
        filled = jnp.zeros_like(lane)
        for p in range(MAXP):
            held = jnp.minimum(jnp.maximum(length - p * PG, 0), PG)
            filled = jnp.where(page == table[place, p], held, filled)
        return jnp.where(inner < filled, 0.0, -1e30)

    def attend(q_rows, new_rows, hidden_bias, first):
        count = q_rows.shape[0]
        heads = range(first, first + count)
        factor = 1.0 / math.sqrt(HD)
        new_keys = jnp.stack([new_rows[j : j + 1] for j in heads])
        new_values = jnp.stack([new_rows[KVH + j : KVH + j + 1] for j in heads])
        q_bf = q_rows.astype(BF)
        score = jnp.stack(
            [
                lax.dot_general(
                    q_bf[j - first], pool_v[:, j * HD : (j + 1) * HD],
                    (((1,), (1,)), ((), ())), preferred_element_type=F32,
                )
                for j in heads
            ]
        )
        score = score * factor + hidden_bias[None]
        own_score = jnp.sum(q_rows * new_keys, axis=-1, keepdims=True) * factor
        top = jnp.maximum(jnp.max(score, axis=-1, keepdims=True), own_score)
        exponent = jnp.exp(score - top)
        own_exponent = jnp.exp(own_score - top)
        scale = 1.0 / (jnp.sum(exponent, axis=-1, keepdims=True) + own_exponent)
        weight = (exponent * scale).astype(BF)
        own_weight = (own_exponent * scale).astype(BF).astype(F32)
        attended = jnp.stack(
            [
                jnp.dot(
                    weight[j - first], pool_v[:, (KVH + j) * HD : (KVH + j + 1) * HD],
                    preferred_element_type=F32,
                )
                for j in heads
            ]
        )
        return attended + own_weight * new_values

    def normalise(res_rows, attended):
        stream = res_rows + attended
        square = jnp.sum(jnp.sum(stream * stream, axis=0), axis=-1, keepdims=True)
        mean = jnp.sum(square, axis=0, keepdims=True) * (1.0 / (DP * 4 * HD))
        scale = lax.rsqrt(mean + EPSILON)
        return stream * scale[None] * gain[...].astype(F32).reshape(KVH, 8, HD), stream

    lines = (line_q, line_res)

    def local(_):
        local_q = q_t[:64].reshape(KVH, 8, HD)
        local_res = res_t[:64].reshape(KVH, 8, HD)
        hidden_bias = bias_of(1 - slot_id)
        use(0)
        normed, stream = normalise(local_res, attend(local_q, new_t[:16], hidden_bias, 0))
        stream_local[...] = stream.reshape(DP * 4, HD)
        for k in range(DP):
            c_local[k] = normed[k // 2, 4 * (k % 2) : 4 * (k % 2) + 4]
        pl.semaphore_wait(barrier, len(partners))
        exchange(c_local, in_local, c_s.at[0], c_r.at[0])
        for i, rows in enumerate(ROUTED):
            for o in range(1, NX):
                place = lax.rem(x + o, NX)
                send(
                    own.at[rows], lines[i].at[x], rx_s.at[i, o - 1], rx_r.at[i, o - 1],
                    (h * NX + place, tp),
                )
            lines[i][x] = own[rows]

    sources = [mig[i, 0, 1] for i in range(MIG)]
    targets = [mig[i, 0, 2] for i in range(MIG)]

    def route(i):
        span_of = ROUTED[i]
        for o in range(1, NX):
            place = lax.rem(x + NX - o, NX)
            arrived(
                lines[i].at[place], rx_s.at[i, o - 1], rx_r.at[i, o - 1],
                (h * NX + place, tp),
            )
        rows = [lines[i][lax.rem(target, NX)].astype(F32) for target in targets]
        here = [lax.div(target, NX) == h for target in targets]

        def wanted(rank):
            value = jnp.zeros_like(rows[0])
            for j in range(MIG):
                value = jnp.where(here[j] & (sources[j] == rank), rows[j], value)
            return value.astype(BF)

        for o in range(1, NH):
            place = lax.rem(h + o, NH)
            y_send[o - 1, span_of] = wanted(place * NX + x)
            send(
                y_send.at[o - 1, span_of], y_recv.at[o - 1, span_of],
                ry_s.at[i, o - 1], ry_r.at[i, o - 1], at_h(place),
            )
        y_recv[NH - 1, span_of] = wanted(dp)

    def routed(i):
        span_of = ROUTED[i]
        for o in range(1, NH):
            arrived(
                y_recv.at[o - 1, span_of], ry_s.at[i, o - 1], ry_r.at[i, o - 1],
                at_h(lax.rem(h + NH - o, NH)),
            )
        row = y_recv[NH - 1, span_of].astype(F32)
        for o in range(NH - 1):
            row = row + y_recv[o, span_of].astype(F32)
        serves = (sources[0] == dp) | (sources[1] == dp) | (sources[2] == dp)
        return jnp.where(serves, row, own[span_of].astype(F32))

    def listed(part):
        if part == 0:
            routed_row[...] = routed(0)
            bias_row[...] = bias_of(slot_id)
        if part < 2:
            q_rows = routed_row[32 * part : 32 * part + 32].reshape(4, 8, HD)
            attended_row[4 * part : 4 * part + 4] = attend(
                q_rows, routed_row[64:], bias_row[...], 4 * part
            )
        else:
            normed, stream = normalise(routed(1).reshape(KVH, 8, HD), attended_row[...])
            even, odd = pieces(normed, stream)
            for k in range(DP):
                c_listed[k] = (even, odd)[k % 2][k // 2]
            exchange(c_listed, in_listed, c_s.at[1], c_r.at[1])

    def start_x(w):
        source, count = (in_local, 4) if w == 0 else (in_listed, 8)
        exchanged(source, c_s.at[w], c_r.at[w])
        for a in range(DP):
            tiles[count * a : count * a + count] = source[a]
        x_all[w, z, c, l] = jnp.concatenate(
            [tiles[pl.ds(i, DP, stride=count), :] for i in range(4)], axis=1
        ).astype(BF)
        block = x_all.at[w, z, c, l]
        send(block, block, xl_s.at[w], xl_r.at[w], across_l)

    def start_y(w):
        arrived(x_all.at[w, z, c, other_l], xl_s.at[w], xl_r.at[w], across_l)
        block = x_all.at[w, z, c]
        send(block, block, xc_s.at[w, 0], xc_r.at[w, 0], across_c)
        offsets = [o for kind, places in CHUNKS if kind == w for o in places if o]
        for o in offsets:
            send(block, block, xz_s.at[w, slot(o)], xz_r.at[w, slot(o)], at_tp(z_at(-o), l, c))

    def forward(q):
        w, offsets = CHUNKS[q]
        for o in offsets:
            if o:
                zz = z_at(o)
                block = x_all.at[w, zz, c]
                arrived(block, xz_s.at[w, slot(o)], xz_r.at[w, slot(o)], at_tp(zz, l, c))
                send(block, block, xc_s.at[w, slot(o)], xc_r.at[w, slot(o)], across_c)

    def span(q):
        return pl.ds(STARTS[q], SIZES[q])

    def stage_a(q):
        w, offsets = CHUNKS[q]
        for o in offsets:
            arrived(x_all.at[w, z_at(o), other_c], xc_s.at[w, slot(o)], xc_r.at[w, slot(o)], across_c)
        use(1)
        use(2)
        rows = jnp.concatenate([x_all[w, z_at(o)].reshape(64, 512) for o in offsets], axis=0)
        part_rows = span(q)
        for weight, dst in ((gate_v, gate_p), (up_v, up_p)):
            value = jnp.dot(rows, weight[...], preferred_element_type=F32).astype(BF)
            dst[:, part_rows] = value.reshape(NX, SIZES[q], 512)
        send(gate_p.at[xo, part_rows], m1g.at[part_rows], xp_s.at[q, 0], xp_r.at[q, 0], right)
        send(up_p.at[xo, part_rows], m1u.at[part_rows], xp_s.at[q, 1], xp_r.at[q, 1], left)
        send(up_p.at[xr, part_rows], m2u.at[part_rows], xp_s.at[q, 2], xp_r.at[q, 2], right)
        send(gate_p.at[xl, part_rows], m2g.at[part_rows], xp_s.at[q, 3], xp_r.at[q, 3], left)

    def stage_b(q):
        t = span(q)
        arrived(m1g.at[t], xp_s.at[q, 0], xp_r.at[q, 0], left)
        s3g[t] = (gate_p[xr, t].astype(F32) + m1g[t].astype(F32)).astype(BF)
        send(s3g.at[t], m3g.at[t], xp_s.at[q, 4], xp_r.at[q, 4], right)
        arrived(m1u.at[t], xp_s.at[q, 1], xp_r.at[q, 1], right)
        s3u[t] = (up_p[xl, t].astype(F32) + m1u[t].astype(F32)).astype(BF)
        send(s3u.at[t], m3u.at[t], xp_s.at[q, 5], xp_r.at[q, 5], left)

    def stage_c(q):
        t = span(q)
        arrived(m2u.at[t], xp_s.at[q, 2], xp_r.at[q, 2], left)
        arrived(m2g.at[t], xp_s.at[q, 3], xp_r.at[q, 3], right)
        arrived(m3g.at[t], xp_s.at[q, 4], xp_r.at[q, 4], left)
        arrived(m3u.at[t], xp_s.at[q, 5], xp_r.at[q, 5], right)
        gate = gate_p[x, t].astype(F32) + m2g[t].astype(F32) + m3g[t].astype(F32)
        up = up_p[x, t].astype(F32) + m2u[t].astype(F32) + m3u[t].astype(F32)
        gate, up = gate.astype(BF), up.astype(BF)
        for b in range(NH):
            columns = slice(b * HD, (b + 1) * HD)
            h_send[b, t] = jnp.concatenate([gate[:, columns], up[:, columns]], axis=1)
        for o in (2, 1, 3):
            place = lax.rem(h + o, NH)
            send(
                h_send.at[place, t], h_recv.at[o - 1, t],
                hp_s.at[q, o - 1], hp_r.at[q, o - 1], at_h(place),
            )

    def stage_d(q):
        t = span(q)
        for o in range(1, NH):
            arrived(
                h_recv.at[o - 1, t], hp_s.at[q, o - 1], hp_r.at[q, o - 1],
                at_h(lax.rem(h + NH - o, NH)),
            )
        total = h_send[h, t].astype(F32)
        for o in range(NH - 1):
            total = total + h_recv[o, t].astype(F32)
        gate, up = total[:, :HD], total[:, HD:]
        hid[x, h, t] = (gate / (1.0 + jnp.exp(-gate)) * up).astype(BF)
        block = hid.at[x, h, t]
        for o in (2, 1, 3):
            send(
                block, block, hg_s.at[q, o - 1], hg_r.at[q, o - 1], at_h(lax.rem(h + o, NH))
            )

    def stage_e(q):
        t = span(q)
        for o in range(1, NH):
            place = lax.rem(h + NH - o, NH)
            arrived(hid.at[x, place, t], hg_s.at[q, o - 1], hg_r.at[q, o - 1], at_h(place))
        block = hid.at[x, pl.ds(0, NH), t]
        send(block, block, xg_s.at[q, 0], xg_r.at[q, 0], right)
        send(block, block, xg_s.at[q, 1], xg_r.at[q, 1], left)

    def stage_f(q):
        t = span(q)
        arrived(hid.at[xl, pl.ds(0, NH), t], xg_s.at[q, 0], xg_r.at[q, 0], left)
        half = hid.at[xl, pl.ds(0, 2), t]
        send(half, half, xg_s.at[q, 2], xg_r.at[q, 2], right)
        arrived(hid.at[xr, pl.ds(0, NH), t], xg_s.at[q, 1], xg_r.at[q, 1], right)
        half = hid.at[xr, pl.ds(2, 2), t]
        send(half, half, xg_s.at[q, 3], xg_r.at[q, 3], left)

    def stage_g(q):
        t = span(q)
        arrived(hid.at[xo, pl.ds(0, 2), t], xg_s.at[q, 2], xg_r.at[q, 2], left)
        arrived(hid.at[xo, pl.ds(2, 2), t], xg_s.at[q, 3], xg_r.at[q, 3], right)
        use(3)
        rows = jnp.concatenate(
            [jnp.concatenate([hid[a, b, t] for b in range(NH)], axis=1) for a in range(NX)], axis=0
        )
        value = jnp.dot(rows, down_v[...], preferred_element_type=F32).astype(BF)
        count, first_block = SIZES[q] // 16, STARTS[q] // 16
        value = value.reshape(count, 2, 2, 16, 512)
        for b in range(count):
            part[:, first_block + b] = value[b]
        blocks = pl.ds(first_block, count)
        send(part.at[other_c, blocks], part_in.at[blocks], oc_s.at[q], oc_r.at[q], across_c)

    def stage_h(q):
        w, offsets = CHUNKS[q]
        first_block = STARTS[q] // 16
        blocks = pl.ds(first_block, SIZES[q] // 16)
        arrived(part_in.at[blocks], oc_s.at[q], oc_r.at[q], across_c)
        z_send[blocks] = (part[c, blocks].astype(F32) + part_in[blocks].astype(F32)).astype(BF)
        for b, o in enumerate(offsets):
            if o:
                send(
                    z_send.at[first_block + b], z_recv.at[w, slot(o)],
                    oz_s.at[w, slot(o)], oz_r.at[w, slot(o)], at_tp(z_at(o), l, c),
                )

    def start_l(w):
        offsets = []
        for q, (kind, places) in enumerate(CHUNKS):
            for b, o in enumerate(places):
                if kind == w and o:
                    offsets.append(o)
                elif kind == w:
                    total = z_send[STARTS[q] // 16 + b].astype(F32)
        for o in offsets:
            arrived(
                z_recv.at[w, slot(o)], oz_s.at[w, slot(o)], oz_r.at[w, slot(o)],
                at_tp(z_at(-o), l, c),
            )
            total = total + z_recv[w, slot(o)].astype(F32)
        l_send[w] = total.astype(BF)
        send(l_send.at[w, other_l], l_recv.at[w], ol_s.at[w], ol_r.at[w], across_l)

    def start_m(w):
        arrived(l_recv.at[w], ol_s.at[w], ol_r.at[w], across_l)
        ffn = l_send[w, l].astype(F32) + l_recv[w].astype(F32)
        for i in range(4):
            rows_out[w, pl.ds(i, DP, stride=4), :] = ffn[:, i * HD : (i + 1) * HD]
        if w == 0:
            for rank in range(DP):
                e_send[0, rank] = rows_out[0, 4 * rank : 4 * rank + 4]
        else:
            for rank in range(DP):
                fin[rank] = rows_out[1, 4 * rank : 4 * rank + 4] + in_listed[rank, 4:]
            for rank in range(DP):
                anchor = jnp.int32(rank)
                for i in range(MIG):
                    anchor = jnp.where(targets[i] == rank, sources[i], anchor)
                e_send[1, rank] = fin[anchor]
        exchange(e_send.at[w], e_recv.at[w], e_s.at[w], e_r.at[w])

    steps = {
        "local": local, "route": route, "listed": listed, "x": start_x, "y": start_y,
        "w": forward, "a": stage_a, "b": stage_b, "c": stage_c, "d": stage_d, "e": stage_e,
        "f": stage_f, "g": stage_g, "h": stage_h, "l": start_l, "m": start_m,
    }
    for step in ORDER:
        name = step.rstrip("0123456789")
        steps[name](int(step[len(name) :] or 0))

    all_left(c_local, c_s.at[0], c_r.at[0])
    all_left(c_listed, c_s.at[1], c_r.at[1])
    for copy in sent:
        copy.wait_send()
    for w in range(2):
        exchanged(e_recv.at[w], e_s.at[w], e_r.at[w])
        for k in range(DP):
            tiles[64 * w + 4 * k : 64 * w + 4 * k + 4] = e_recv[w, k]
    tiles[:64] = tiles[:64] + stream_local[...]
    stays, moved = tiles[:64], tiles[64:]
    out[:64] = jnp.where(second, stays, moved)
    out[64:] = jnp.where(second, moved, stays)
    for w in range(2):
        all_left(e_send.at[w], e_s.at[w], e_r.at[w])


def on_device(
    queries, residual, new_entries, page_pool, page_table, cache_lengths, migration,
    norm_gain, gate_weight, up_weight, down_weight,
):
    pages, page_rows, entry = page_pool.shape[2:]
    vmem = pl.BlockSpec(memory_space=pltpu.VMEM)
    hbm = pl.BlockSpec(memory_space=pl.ANY)
    smem = pl.BlockSpec(memory_space=pltpu.SMEM)
    nq = len(CHUNKS)
    dma = pltpu.SemaphoreType.DMA
    share = (256, 512)
    scratch = [
        pltpu.VMEM((512, 2048), BF),
        pltpu.VMEM((512, 512), BF), pltpu.VMEM((512, 512), BF), pltpu.VMEM((512, 512), BF),
        pltpu.VMEM((128, HD), F32), pltpu.VMEM((128, HD), F32), pltpu.VMEM((32, HD), F32),
        pltpu.VMEM((144, HD), BF), pltpu.VMEM((NX, 80, HD), BF), pltpu.VMEM((NX, 64, HD), BF),
        pltpu.VMEM((NH - 1, 144, HD), BF), pltpu.VMEM((NH, 144, HD), BF),
        pltpu.VMEM((DP, 4, HD), F32), pltpu.VMEM((DP, 8, HD), F32),
        pltpu.VMEM((DP, 4, HD), F32), pltpu.VMEM((DP, 8, HD), F32),
        pltpu.VMEM((64, HD), F32), pltpu.VMEM((80, HD), F32), pltpu.VMEM((KVH, 8, HD), F32),
        pltpu.VMEM((8, MAXP * 2 * PG), F32), pltpu.VMEM((DP * 8, HD), F32),
        pltpu.VMEM((2, NZ, 2, 2, 16, 512), BF),
        pltpu.VMEM((NX,) + share, BF), pltpu.VMEM((NX,) + share, BF),
    ]
    scratch += [pltpu.VMEM(share, BF) for _ in range(8)]
    scratch += [
        pltpu.VMEM((NH, 256, 256), BF), pltpu.VMEM((NH - 1, 256, 256), BF),
        pltpu.VMEM((NX, NH, 256, HD), BF),
        pltpu.VMEM((2, 16, 2, 16, 512), BF), pltpu.VMEM((16, 2, 16, 512), BF),
        pltpu.VMEM((16, 2, 16, 512), BF), pltpu.VMEM((2, NZ, 2, 16, 512), BF),
        pltpu.VMEM((2, 2, 16, 512), BF), pltpu.VMEM((2, 16, 512), BF),
        pltpu.VMEM((2, 64, HD), F32), pltpu.VMEM((DP, 4, HD), F32),
        pltpu.VMEM((2, DP, 4, HD), F32), pltpu.VMEM((2, DP, 4, HD), F32),
    ]
    scratch += [dma((4,))]
    scratch += [dma((2, 3)) for _ in range(4)]
    scratch += [dma((2,)), dma((2,)), dma((2,)), dma((2,))]
    scratch += [dma((2,)), dma((2,)), dma((2, NZ)), dma((2, NZ)), dma((2, NZ)), dma((2, NZ))]
    scratch += [dma((nq, 6)), dma((nq, 6)), dma((nq, 3)), dma((nq, 3)), dma((nq, 3)), dma((nq, 3))]
    scratch += [dma((nq, 4)), dma((nq, 4)), dma((nq,)), dma((nq,)), dma((2, NZ)), dma((2, NZ))]
    scratch += [dma((2,)), dma((2,))]
    done = pl.pallas_call(
        kernel,
        out_shape=jax.ShapeDtypeStruct((2 * DP * 4, HD), F32),
        in_specs=[smem, smem, smem, vmem, vmem, vmem, vmem, hbm, hbm, hbm, hbm],
        out_specs=vmem,
        scratch_shapes=scratch,
        compiler_params=pltpu.CompilerParams(
            collective_id=0, has_side_effects=True, vmem_limit_bytes=62 * 1024 * 1024
        ),
    )(
        migration.transpose(1, 0, 2), page_table[0, 0], cache_lengths[0, 0],
        queries[0, 0], residual[0, 0], new_entries[0, 0], norm_gain.reshape(DP * 4, HD),
        page_pool.reshape(pages * page_rows, entry), gate_weight, up_weight, down_weight,
    )
    return done.reshape(1, 1, 2, DP * 4 * HD).astype(BF)


def solution(mesh):
    return jax.shard_map(
        on_device,
        mesh=mesh,
        in_specs=(
            P("dp", "tp", None, None),
            P("dp", "tp", None, None),
            P("dp", "tp", None, None),
            P("dp", "tp", None, None, None),
            P("dp", "tp", None, None),
            P("dp", "tp", None),
            P("tp", None, None),
            P(),
            P("dp", "tp"),
            P("dp", "tp"),
            P("tp", "dp"),
        ),
        out_specs=P("dp", "tp", None, None),
        check_vma=False,
    )
```

```python
import math

import jax
import jax.numpy as jnp
from jax import lax
from jax.experimental import pallas as pl
from jax.experimental.pallas import tpu as pltpu
from jax.sharding import PartitionSpec as P

HD = 128
KVH = 8
NX, NH, NZ = 4, 4, 8
DP = NX * NH
MIG = 3
MAXP, PG = 16, 16
CHUNKS = (
    (0, (0, 1)), (0, (-1, 2)), (0, (-2, 3)), (0, (-3, 4)),
    (1, (-3, 4)), (1, (-2, 3)), (1, (-1, 2)), (1, (0, 1)),
)
SIZES = [16 * len(offsets) for _, offsets in CHUNKS]
STARTS = [sum(SIZES[:q]) for q in range(len(CHUNKS))]
ORDER = (
    "local", "x0", "route0", "route1", "y0", "listed0", "listed1", "w0", "listed2", "w2", "a0",
    "w1", "a2", "x1", "w3", "b0", "a1", "y1", "b1", "c0", "b2", "a3", "c1", "w4", "c2", "b3",
    "w5", "d0", "a4", "w6", "a5", "c3", "d2", "a6", "w7", "d1", "b5", "b4", "b6", "e0", "d3",
    "a7", "c5", "e2", "c4", "f0", "b7", "c6", "f2", "e1", "d5", "e3", "d4", "g2", "c7", "f1",
    "f3", "e5", "g0", "h2", "e4", "d6", "d7", "g3", "f4", "f5", "e6", "g1", "h3", "e7", "g4",
    "h0", "h1", "f6", "g5", "f7", "h4", "g6", "h5", "l0", "g7", "h6", "h7", "m0", "l1", "m1",
)
ROUTED = (pl.ds(0, 80), pl.ds(80, 64))
DISTANCES = (10, 9, 11, 8, 6, 14, 2, 5, 7, 13, 15, 4, 12, 1, 3)
LAG = 16
EPSILON = 1e-05
BF = jnp.bfloat16
F32 = jnp.float32


def kernel(
    mig, table, lengths, q_in, res_in, new_in, gain, pool, gate_w, up_w, down_w, out,
    pool_v, gate_v, up_v, down_v,
    q_t, res_t, new_t, own, line_q, line_res, y_send, y_recv, c_local, c_listed, in_local, in_listed,
    stream_local, routed_row, attended_row, bias_row, tiles, x_all,
    gate_p, up_p, m1g, m1u, m2g, m2u, s3g, s3u, m3g, m3u,
    h_send, h_recv, hid, part, part_in, z_send, z_recv, l_send, l_recv,
    rows_out, fin, e_send, e_recv,
    load_sem, rx_s, rx_r, ry_s, ry_r, c_s, c_r, e_s, e_r,
    xl_s, xl_r, xz_s, xz_r, xc_s, xc_r,
    xp_s, xp_r, hp_s, hp_r, hg_s, hg_r, xg_s, xg_r,
    oc_s, oc_r, oz_s, oz_r, ol_s, ol_r,
):
    dp, tp = lax.axis_index("dp"), lax.axis_index("tp")
    h, x = lax.div(dp, NX), lax.rem(dp, NX)
    z, low = lax.div(tp, 4), lax.rem(tp, 4)
    l, c = lax.div(low, 2), lax.rem(low, 2)
    other_l, other_c = 1 - l, 1 - c
    xr, xo, xl = lax.rem(x + 1, NX), lax.rem(x + 2, NX), lax.rem(x + 3, NX)
    right, left = (h * NX + xr, tp), (h * NX + xl, tp)

    def at_dp(rank):
        return (rank, tp)

    def at_h(place):
        return (place * NX + x, tp)

    def at_tp(zz, ll, cc):
        return (dp, zz * 4 + ll * 2 + cc)

    def z_at(offset):
        return lax.rem(z + (offset + NZ), NZ)

    def slot(offset):
        return (offset + NZ) % NZ

    across_l, across_c = at_tp(z, other_l, c), at_tp(z, l, other_c)
    sent = []

    def send(src, dst, send_sem, recv_sem, device, listed_copy=True):
        copy = pltpu.make_async_remote_copy(
            src_ref=src, dst_ref=dst, send_sem=send_sem, recv_sem=recv_sem,
            device_id=device, device_id_type=pl.DeviceIdType.MESH,
        )
        copy.start()
        if listed_copy:
            sent.append(copy)

    def arrived(dst, send_sem, recv_sem, device):
        pltpu.make_async_remote_copy(
            src_ref=dst, dst_ref=dst, send_sem=send_sem, recv_sem=recv_sem,
            device_id=device, device_id_type=pl.DeviceIdType.MESH,
        ).wait_recv()

    loads = [
        pltpu.make_async_copy(src, dst, load_sem.at[i])
        for i, (src, dst) in enumerate(
            ((pool, pool_v), (gate_w, gate_v), (up_w, up_v), (down_w, down_v))
        )
    ]
    for copy in loads:
        copy.start()
    waiting = set(range(len(loads)))

    def use(i):
        if i in waiting:
            waiting.discard(i)
            loads[i].wait()


    others = [lax.rem(h + o // NX, NH) * NX + lax.rem(x + o % NX, NX) for o in DISTANCES]
    barrier = pltpu.get_barrier_semaphore()
    partners = [at_dp(rank) for rank in others]
    partners += [at_tp(z_at(o), l, c) for o in range(1, NZ)] + [across_l, across_c]
    for device in partners:
        pl.semaphore_signal(barrier, inc=1, device_id=device, device_id_type=pl.DeviceIdType.MESH)

    def exchange(src, dst, s_sem, r_sem):
        for rank in others:
            send(src.at[rank], dst.at[dp], s_sem, r_sem, at_dp(rank), False)
        dst[dp] = src[dp]

    def exchanged(dst, s_sem, r_sem):
        arrived(dst.at[pl.ds(0, DP - 1)], s_sem, r_sem, at_dp(others[0]))

    def all_left(src, s_sem, r_sem):
        part = src.at[pl.ds(0, DP - 1)]
        pltpu.make_async_remote_copy(
            src_ref=part, dst_ref=part, send_sem=s_sem, recv_sem=r_sem,
            device_id=at_dp(others[0]), device_id_type=pl.DeviceIdType.MESH,
        ).wait_send()

    slot_id = mig[0, 0, 0]
    second = slot_id == 1

    def ordered(value):
        return jnp.where(second, value, jnp.concatenate([value[1:2], value[0:1]], axis=0))

    for source, dst, count in ((q_in, q_t, 64), (res_in, res_t, 64), (new_in, new_t, 16)):
        value = ordered(source[...].astype(F32))
        for j in range(count):
            dst[pl.ds(j, 2, stride=count), :] = value[:, j * HD : (j + 1) * HD]

    top_half = lax.broadcasted_iota(jnp.int32, (KVH, 8, HD), 1) < 4

    def turned(value):
        return jnp.concatenate([value[:, 4:], value[:, :4]], axis=1)

    def pieces(first, second_value):
        even = jnp.where(top_half, first, turned(second_value))
        odd = jnp.where(top_half, turned(first), second_value)
        return even, odd

    own[...] = jnp.concatenate([q_t[64:], new_t[16:], res_t[64:]], axis=0).astype(BF)

    def bias_of(place):
        lane = lax.broadcasted_iota(jnp.int32, (8, MAXP * 2 * PG), 1)
        page, inner = lane >> 4, lane & 15
        length = lengths[place]
        filled = jnp.zeros_like(lane)
        for p in range(MAXP):
            held = jnp.minimum(jnp.maximum(length - p * PG, 0), PG)
            filled = jnp.where(page == table[place, p], held, filled)
        return jnp.where(inner < filled, 0.0, -1e30)

    def attend(q_rows, new_rows, hidden_bias, first):
        count = q_rows.shape[0]
        heads = range(first, first + count)
        factor = 1.0 / math.sqrt(HD)
        new_keys = jnp.stack([new_rows[j : j + 1] for j in heads])
        new_values = jnp.stack([new_rows[KVH + j : KVH + j + 1] for j in heads])
        q_bf = q_rows.astype(BF)
        score = jnp.stack(
            [
                lax.dot_general(
                    q_bf[j - first], pool_v[:, j * HD : (j + 1) * HD],
                    (((1,), (1,)), ((), ())), preferred_element_type=F32,
                )
                for j in heads
            ]
        )
        score = score * factor + hidden_bias[None]
        own_score = jnp.sum(q_rows * new_keys, axis=-1, keepdims=True) * factor
        top = jnp.maximum(jnp.max(score, axis=-1, keepdims=True), own_score)
        exponent = jnp.exp(score - top)
        own_exponent = jnp.exp(own_score - top)
        scale = 1.0 / (jnp.sum(exponent, axis=-1, keepdims=True) + own_exponent)
        weight = (exponent * scale).astype(BF)
        own_weight = (own_exponent * scale).astype(BF).astype(F32)
        attended = jnp.stack(
            [
                jnp.dot(
                    weight[j - first], pool_v[:, (KVH + j) * HD : (KVH + j + 1) * HD],
                    preferred_element_type=F32,
                )
                for j in heads
            ]
        )
        return attended + own_weight * new_values

    def normalise(res_rows, attended):
        stream = res_rows + attended
        square = jnp.sum(jnp.sum(stream * stream, axis=0), axis=-1, keepdims=True)
        mean = jnp.sum(square, axis=0, keepdims=True) * (1.0 / (DP * 4 * HD))
        scale = lax.rsqrt(mean + EPSILON)
        return stream * scale[None] * gain[...].astype(F32).reshape(KVH, 8, HD), stream

    lines = (line_q, line_res)

    def local(_):
        local_q = q_t[:64].reshape(KVH, 8, HD)
        local_res = res_t[:64].reshape(KVH, 8, HD)
        hidden_bias = bias_of(1 - slot_id)
        use(0)
        normed, stream = normalise(local_res, attend(local_q, new_t[:16], hidden_bias, 0))
        stream_local[...] = stream.reshape(DP * 4, HD)
        for k in range(DP):
            c_local[k] = normed[k // 2, 4 * (k % 2) : 4 * (k % 2) + 4]
        pl.semaphore_wait(barrier, len(partners))
        exchange(c_local, in_local, c_s.at[0], c_r.at[0])
        for i, rows in enumerate(ROUTED):
            for o in range(1, NX):
                place = lax.rem(x + o, NX)
                send(
                    own.at[rows], lines[i].at[x], rx_s.at[i, o - 1], rx_r.at[i, o - 1],
                    (h * NX + place, tp),
                )
            lines[i][x] = own[rows]

    sources = [mig[i, 0, 1] for i in range(MIG)]
    targets = [mig[i, 0, 2] for i in range(MIG)]

    def route(i):
        span_of = ROUTED[i]
        for o in range(1, NX):
            place = lax.rem(x + NX - o, NX)
            arrived(
                lines[i].at[place], rx_s.at[i, o - 1], rx_r.at[i, o - 1],
                (h * NX + place, tp),
            )
        rows = [lines[i][lax.rem(target, NX)].astype(F32) for target in targets]
        here = [lax.div(target, NX) == h for target in targets]

        def wanted(rank):
            value = jnp.zeros_like(rows[0])
            for j in range(MIG):
                value = jnp.where(here[j] & (sources[j] == rank), rows[j], value)
            return value.astype(BF)

        for o in range(1, NH):
            place = lax.rem(h + o, NH)
            y_send[o - 1, span_of] = wanted(place * NX + x)
            send(
                y_send.at[o - 1, span_of], y_recv.at[o - 1, span_of],
                ry_s.at[i, o - 1], ry_r.at[i, o - 1], at_h(place),
            )
        y_recv[NH - 1, span_of] = wanted(dp)

    def routed(i):
        span_of = ROUTED[i]
        for o in range(1, NH):
            arrived(
                y_recv.at[o - 1, span_of], ry_s.at[i, o - 1], ry_r.at[i, o - 1],
                at_h(lax.rem(h + NH - o, NH)),
            )
        row = y_recv[NH - 1, span_of].astype(F32)
        for o in range(NH - 1):
            row = row + y_recv[o, span_of].astype(F32)
        serves = (sources[0] == dp) | (sources[1] == dp) | (sources[2] == dp)
        return jnp.where(serves, row, own[span_of].astype(F32))

    def listed(part):
        if part == 0:
            routed_row[...] = routed(0)
            bias_row[...] = bias_of(slot_id)
        if part < 2:
            q_rows = routed_row[32 * part : 32 * part + 32].reshape(4, 8, HD)
            attended_row[4 * part : 4 * part + 4] = attend(
                q_rows, routed_row[64:], bias_row[...], 4 * part
            )
        else:
            normed, stream = normalise(routed(1).reshape(KVH, 8, HD), attended_row[...])
            even, odd = pieces(normed, stream)
            for k in range(DP):
                c_listed[k] = (even, odd)[k % 2][k // 2]
            exchange(c_listed, in_listed, c_s.at[1], c_r.at[1])

    def start_x(w):
        source, count = (in_local, 4) if w == 0 else (in_listed, 8)
        exchanged(source, c_s.at[w], c_r.at[w])
        for a in range(DP):
            tiles[count * a : count * a + count] = source[a]
        x_all[w, z, c, l] = jnp.concatenate(
            [tiles[pl.ds(i, DP, stride=count), :] for i in range(4)], axis=1
        ).astype(BF)
        block = x_all.at[w, z, c, l]
        send(block, block, xl_s.at[w], xl_r.at[w], across_l)

    def start_y(w):
        arrived(x_all.at[w, z, c, other_l], xl_s.at[w], xl_r.at[w], across_l)
        block = x_all.at[w, z, c]
        send(block, block, xc_s.at[w, 0], xc_r.at[w, 0], across_c)
        offsets = [o for kind, places in CHUNKS if kind == w for o in places if o]
        for o in offsets:
            send(block, block, xz_s.at[w, slot(o)], xz_r.at[w, slot(o)], at_tp(z_at(-o), l, c))

    def forward(q):
        w, offsets = CHUNKS[q]
        for o in offsets:
            if o:
                zz = z_at(o)
                block = x_all.at[w, zz, c]
                arrived(block, xz_s.at[w, slot(o)], xz_r.at[w, slot(o)], at_tp(zz, l, c))
                send(block, block, xc_s.at[w, slot(o)], xc_r.at[w, slot(o)], across_c)

    def span(q):
        return pl.ds(STARTS[q], SIZES[q])

    def stage_a(q):
        w, offsets = CHUNKS[q]
        for o in offsets:
            arrived(x_all.at[w, z_at(o), other_c], xc_s.at[w, slot(o)], xc_r.at[w, slot(o)], across_c)
        use(1)
        use(2)
        rows = jnp.concatenate([x_all[w, z_at(o)].reshape(64, 512) for o in offsets], axis=0)
        part_rows = span(q)
        for weight, dst in ((gate_v, gate_p), (up_v, up_p)):
            value = jnp.dot(rows, weight[...], preferred_element_type=F32).astype(BF)
            dst[:, part_rows] = value.reshape(NX, SIZES[q], 512)
        send(gate_p.at[xo, part_rows], m1g.at[part_rows], xp_s.at[q, 0], xp_r.at[q, 0], right)
        send(up_p.at[xo, part_rows], m1u.at[part_rows], xp_s.at[q, 1], xp_r.at[q, 1], left)
        send(up_p.at[xr, part_rows], m2u.at[part_rows], xp_s.at[q, 2], xp_r.at[q, 2], right)
        send(gate_p.at[xl, part_rows], m2g.at[part_rows], xp_s.at[q, 3], xp_r.at[q, 3], left)

    def stage_b(q):
        t = span(q)
        arrived(m1g.at[t], xp_s.at[q, 0], xp_r.at[q, 0], left)
        s3g[t] = (gate_p[xr, t].astype(F32) + m1g[t].astype(F32)).astype(BF)
        send(s3g.at[t], m3g.at[t], xp_s.at[q, 4], xp_r.at[q, 4], right)
        arrived(m1u.at[t], xp_s.at[q, 1], xp_r.at[q, 1], right)
        s3u[t] = (up_p[xl, t].astype(F32) + m1u[t].astype(F32)).astype(BF)
        send(s3u.at[t], m3u.at[t], xp_s.at[q, 5], xp_r.at[q, 5], left)

    def stage_c(q):
        t = span(q)
        arrived(m2u.at[t], xp_s.at[q, 2], xp_r.at[q, 2], left)
        arrived(m2g.at[t], xp_s.at[q, 3], xp_r.at[q, 3], right)
        arrived(m3g.at[t], xp_s.at[q, 4], xp_r.at[q, 4], left)
        arrived(m3u.at[t], xp_s.at[q, 5], xp_r.at[q, 5], right)
        gate = gate_p[x, t].astype(F32) + m2g[t].astype(F32) + m3g[t].astype(F32)
        up = up_p[x, t].astype(F32) + m2u[t].astype(F32) + m3u[t].astype(F32)
        gate, up = gate.astype(BF), up.astype(BF)
        for b in range(NH):
            columns = slice(b * HD, (b + 1) * HD)
            h_send[b, t] = jnp.concatenate([gate[:, columns], up[:, columns]], axis=1)
        for o in (2, 1, 3):
            place = lax.rem(h + o, NH)
            send(
                h_send.at[place, t], h_recv.at[o - 1, t],
                hp_s.at[q, o - 1], hp_r.at[q, o - 1], at_h(place),
            )

    def stage_d(q):
        t = span(q)
        for o in range(1, NH):
            arrived(
                h_recv.at[o - 1, t], hp_s.at[q, o - 1], hp_r.at[q, o - 1],
                at_h(lax.rem(h + NH - o, NH)),
            )
        total = h_send[h, t].astype(F32)
        for o in range(NH - 1):
            total = total + h_recv[o, t].astype(F32)
        gate, up = total[:, :HD], total[:, HD:]
        hid[x, h, t] = (gate / (1.0 + jnp.exp(-gate)) * up).astype(BF)
        block = hid.at[x, h, t]
        for o in (2, 1, 3):
            send(
                block, block, hg_s.at[q, o - 1], hg_r.at[q, o - 1], at_h(lax.rem(h + o, NH))
            )

    def stage_e(q):
        t = span(q)
        for o in range(1, NH):
            place = lax.rem(h + NH - o, NH)
            arrived(hid.at[x, place, t], hg_s.at[q, o - 1], hg_r.at[q, o - 1], at_h(place))
        block = hid.at[x, pl.ds(0, NH), t]
        send(block, block, xg_s.at[q, 0], xg_r.at[q, 0], right)
        send(block, block, xg_s.at[q, 1], xg_r.at[q, 1], left)

    def stage_f(q):
        t = span(q)
        arrived(hid.at[xl, pl.ds(0, NH), t], xg_s.at[q, 0], xg_r.at[q, 0], left)
        half = hid.at[xl, pl.ds(0, 2), t]
        send(half, half, xg_s.at[q, 2], xg_r.at[q, 2], right)
        arrived(hid.at[xr, pl.ds(0, NH), t], xg_s.at[q, 1], xg_r.at[q, 1], right)
        half = hid.at[xr, pl.ds(2, 2), t]
        send(half, half, xg_s.at[q, 3], xg_r.at[q, 3], left)

    def stage_g(q):
        t = span(q)
        arrived(hid.at[xo, pl.ds(0, 2), t], xg_s.at[q, 2], xg_r.at[q, 2], left)
        arrived(hid.at[xo, pl.ds(2, 2), t], xg_s.at[q, 3], xg_r.at[q, 3], right)
        use(3)
        rows = jnp.concatenate(
            [jnp.concatenate([hid[a, b, t] for b in range(NH)], axis=1) for a in range(NX)], axis=0
        )
        value = jnp.dot(rows, down_v[...], preferred_element_type=F32).astype(BF)
        count, first_block = SIZES[q] // 16, STARTS[q] // 16
        value = value.reshape(count, 2, 2, 16, 512)
        for b in range(count):
            part[:, first_block + b] = value[b]
        blocks = pl.ds(first_block, count)
        send(part.at[other_c, blocks], part_in.at[blocks], oc_s.at[q], oc_r.at[q], across_c)

    def stage_h(q):
        w, offsets = CHUNKS[q]
        first_block = STARTS[q] // 16
        blocks = pl.ds(first_block, SIZES[q] // 16)
        arrived(part_in.at[blocks], oc_s.at[q], oc_r.at[q], across_c)
        z_send[blocks] = (part[c, blocks].astype(F32) + part_in[blocks].astype(F32)).astype(BF)
        for b, o in enumerate(offsets):
            if o:
                send(
                    z_send.at[first_block + b], z_recv.at[w, slot(o)],
                    oz_s.at[w, slot(o)], oz_r.at[w, slot(o)], at_tp(z_at(o), l, c),
                )

    def start_l(w):
        offsets = []
        for q, (kind, places) in enumerate(CHUNKS):
            for b, o in enumerate(places):
                if kind == w and o:
                    offsets.append(o)
                elif kind == w:
                    total = z_send[STARTS[q] // 16 + b].astype(F32)
        for o in offsets:
            arrived(
                z_recv.at[w, slot(o)], oz_s.at[w, slot(o)], oz_r.at[w, slot(o)],
                at_tp(z_at(-o), l, c),
            )
            total = total + z_recv[w, slot(o)].astype(F32)
        l_send[w] = total.astype(BF)
        send(l_send.at[w, other_l], l_recv.at[w], ol_s.at[w], ol_r.at[w], across_l)

    def start_m(w):
        arrived(l_recv.at[w], ol_s.at[w], ol_r.at[w], across_l)
        ffn = l_send[w, l].astype(F32) + l_recv[w].astype(F32)
        for i in range(4):
            rows_out[w, pl.ds(i, DP, stride=4), :] = ffn[:, i * HD : (i + 1) * HD]
        if w == 0:
            for rank in range(DP):
                e_send[0, rank] = rows_out[0, 4 * rank : 4 * rank + 4]
        else:
            for rank in range(DP):
                fin[rank] = rows_out[1, 4 * rank : 4 * rank + 4] + in_listed[rank, 4:]
            for rank in range(DP):
                anchor = jnp.int32(rank)
                for i in range(MIG):
                    anchor = jnp.where(targets[i] == rank, sources[i], anchor)
                e_send[1, rank] = fin[anchor]
        exchange(e_send.at[w], e_recv.at[w], e_s.at[w], e_r.at[w])

    steps = {
        "local": local, "route": route, "listed": listed, "x": start_x, "y": start_y,
        "w": forward, "a": stage_a, "b": stage_b, "c": stage_c, "d": stage_d, "e": stage_e,
        "f": stage_f, "g": stage_g, "h": stage_h, "l": start_l, "m": start_m,
    }
    counts, left_behind = [], 0
    for step in ORDER:
        name = step.rstrip("0123456789")
        steps[name](int(step[len(name) :] or 0))
        counts.append(len(sent))
        if len(counts) > LAG:
            while left_behind < counts[-LAG]:
                sent[left_behind].wait_send()
                left_behind += 1

    all_left(c_local, c_s.at[0], c_r.at[0])
    all_left(c_listed, c_s.at[1], c_r.at[1])
    for copy in sent[left_behind:]:
        copy.wait_send()
    for w in range(2):
        exchanged(e_recv.at[w], e_s.at[w], e_r.at[w])
        for k in range(DP):
            tiles[64 * w + 4 * k : 64 * w + 4 * k + 4] = e_recv[w, k]
    tiles[:64] = tiles[:64] + stream_local[...]
    stays, moved = tiles[:64], tiles[64:]
    out[:64] = jnp.where(second, stays, moved).astype(BF)
    out[64:] = jnp.where(second, moved, stays).astype(BF)
    for w in range(2):
        all_left(e_send.at[w], e_s.at[w], e_r.at[w])


def on_device(
    queries, residual, new_entries, page_pool, page_table, cache_lengths, migration,
    norm_gain, gate_weight, up_weight, down_weight,
):
    pages, page_rows, entry = page_pool.shape[2:]
    vmem = pl.BlockSpec(memory_space=pltpu.VMEM)
    hbm = pl.BlockSpec(memory_space=pl.ANY)
    smem = pl.BlockSpec(memory_space=pltpu.SMEM)
    nq = len(CHUNKS)
    dma = pltpu.SemaphoreType.DMA
    share = (256, 512)
    scratch = [
        pltpu.VMEM((512, 2048), BF),
        pltpu.VMEM((512, 512), BF), pltpu.VMEM((512, 512), BF), pltpu.VMEM((512, 512), BF),
        pltpu.VMEM((128, HD), F32), pltpu.VMEM((128, HD), F32), pltpu.VMEM((32, HD), F32),
        pltpu.VMEM((144, HD), BF), pltpu.VMEM((NX, 80, HD), BF), pltpu.VMEM((NX, 64, HD), BF),
        pltpu.VMEM((NH - 1, 144, HD), BF), pltpu.VMEM((NH, 144, HD), BF),
        pltpu.VMEM((DP, 4, HD), F32), pltpu.VMEM((DP, 8, HD), F32),
        pltpu.VMEM((DP, 4, HD), F32), pltpu.VMEM((DP, 8, HD), F32),
        pltpu.VMEM((64, HD), F32), pltpu.VMEM((80, HD), F32), pltpu.VMEM((KVH, 8, HD), F32),
        pltpu.VMEM((8, MAXP * 2 * PG), F32), pltpu.VMEM((DP * 8, HD), F32),
        pltpu.VMEM((2, NZ, 2, 2, 16, 512), BF),
        pltpu.VMEM((NX,) + share, BF), pltpu.VMEM((NX,) + share, BF),
    ]
    scratch += [pltpu.VMEM(share, BF) for _ in range(8)]
    scratch += [
        pltpu.VMEM((NH, 256, 256), BF), pltpu.VMEM((NH - 1, 256, 256), BF),
        pltpu.VMEM((NX, NH, 256, HD), BF),
        pltpu.VMEM((2, 16, 2, 16, 512), BF), pltpu.VMEM((16, 2, 16, 512), BF),
        pltpu.VMEM((16, 2, 16, 512), BF), pltpu.VMEM((2, NZ, 2, 16, 512), BF),
        pltpu.VMEM((2, 2, 16, 512), BF), pltpu.VMEM((2, 16, 512), BF),
        pltpu.VMEM((2, 64, HD), F32), pltpu.VMEM((DP, 4, HD), F32),
        pltpu.VMEM((2, DP, 4, HD), F32), pltpu.VMEM((2, DP, 4, HD), F32),
    ]
    scratch += [dma((4,))]
    scratch += [dma((2, 3)) for _ in range(4)]
    scratch += [dma((2,)), dma((2,)), dma((2,)), dma((2,))]
    scratch += [dma((2,)), dma((2,)), dma((2, NZ)), dma((2, NZ)), dma((2, NZ)), dma((2, NZ))]
    scratch += [dma((nq, 6)), dma((nq, 6)), dma((nq, 3)), dma((nq, 3)), dma((nq, 3)), dma((nq, 3))]
    scratch += [dma((nq, 4)), dma((nq, 4)), dma((nq,)), dma((nq,)), dma((2, NZ)), dma((2, NZ))]
    scratch += [dma((2,)), dma((2,))]
    done = pl.pallas_call(
        kernel,
        out_shape=jax.ShapeDtypeStruct((2 * DP * 4, HD), BF),
        in_specs=[smem, smem, smem, vmem, vmem, vmem, vmem, hbm, hbm, hbm, hbm],
        out_specs=vmem,
        scratch_shapes=scratch,
        compiler_params=pltpu.CompilerParams(
            collective_id=0, has_side_effects=True, vmem_limit_bytes=62 * 1024 * 1024
        ),
    )(
        migration.transpose(1, 0, 2), page_table[0, 0], cache_lengths[0, 0],
        queries[0, 0], residual[0, 0], new_entries[0, 0], norm_gain.reshape(DP * 4, HD),
        page_pool.reshape(pages * page_rows, entry), gate_weight, up_weight, down_weight,
    )
    return done.reshape(1, 1, 2, DP * 4 * HD)


def solution(mesh):
    return jax.shard_map(
        on_device,
        mesh=mesh,
        in_specs=(
            P("dp", "tp", None, None),
            P("dp", "tp", None, None),
            P("dp", "tp", None, None),
            P("dp", "tp", None, None, None),
            P("dp", "tp", None, None),
            P("dp", "tp", None),
            P("tp", None, None),
            P(),
            P("dp", "tp"),
            P("dp", "tp"),
            P("tp", "dp"),
        ),
        out_specs=P("dp", "tp", None, None),
        check_vma=False,
    )
```

```python
import math

import jax
import jax.numpy as jnp
from jax import lax
from jax.experimental import pallas as pl
from jax.experimental.pallas import tpu as pltpu
from jax.sharding import PartitionSpec as P

HD = 128
KVH = 8
NX, NH, NZ = 4, 4, 8
DP = NX * NH
MIG = 3
MAXP, PG = 16, 16
CHUNKS = (
    (0, (0, 1)), (0, (-1, 2)), (0, (-2, 3)), (0, (-3, 4)),
    (1, (-3, 4)), (1, (-2, 3)), (1, (-1, 2)), (1, (0, 1)),
)
SIZES = [16 * len(offsets) for _, offsets in CHUNKS]
STARTS = [sum(SIZES[:q]) for q in range(len(CHUNKS))]
ORDER = (
    "local", "x0", "route0", "route1", "y0", "listed0", "listed1", "w0", "listed2", "w2", "a0",
    "w1", "a2", "x1", "w3", "b0", "a1", "y1", "b1", "c0", "b2", "a3", "c1", "w4", "c2", "b3",
    "w5", "d0", "a4", "w6", "a5", "c3", "d2", "a6", "w7", "d1", "b5", "b4", "b6", "e0", "d3",
    "a7", "c5", "e2", "c4", "f0", "b7", "c6", "f2", "e1", "d5", "e3", "d4", "g2", "c7", "f1",
    "f3", "e5", "g0", "h2", "e4", "d6", "d7", "g3", "f4", "f5", "e6", "g1", "h3", "e7", "g4",
    "h0", "h1", "f6", "g5", "f7", "h4", "g6", "h5", "l0", "g7", "h6", "h7", "m0", "l1", "m1",
)
ROUTED = (pl.ds(0, 80), pl.ds(80, 64))
DISTANCES = (10, 9, 11, 8, 6, 14, 2, 5, 7, 13, 15, 4, 12, 1, 3)
LAG = 16
EPSILON = 1e-05
BF = jnp.bfloat16
F32 = jnp.float32


def kernel(
    mig, table, lengths, q_in, res_in, new_in, gain, pool, gate_w, up_w, down_w, out,
    pool_v, gate_v, up_v, down_v,
    q_t, res_t, new_t, own, line_q, line_res, y_send, y_recv, c_local, c_listed, in_local, in_listed,
    stream_local, routed_row, attended_row, bias_row, tiles, x_all,
    gate_p, up_p, m1g, m1u, m2g, m2u, s3g, s3u, m3g, m3u,
    h_send, h_recv, hid, part, part_in, z_send, z_recv, l_send, l_recv,
    rows_out, fin, e_send, e_recv,
    load_sem, rx_s, rx_r, ry_s, ry_r, c_s, c_r, e_s, e_r,
    xl_s, xl_r, xz_s, xz_r, xc_s, xc_r,
    xp_s, xp_r, hp_s, hp_r, hg_s, hg_r, xg_s, xg_r,
    oc_s, oc_r, oz_s, oz_r, ol_s, ol_r,
):
    dp, tp = lax.axis_index("dp"), lax.axis_index("tp")
    h, x = lax.div(dp, NX), lax.rem(dp, NX)
    z, low = lax.div(tp, 4), lax.rem(tp, 4)
    l, c = lax.div(low, 2), lax.rem(low, 2)
    other_l, other_c = 1 - l, 1 - c
    xr, xo, xl = lax.rem(x + 1, NX), lax.rem(x + 2, NX), lax.rem(x + 3, NX)
    right, left = (h * NX + xr, tp), (h * NX + xl, tp)

    def at_dp(rank):
        return (rank, tp)

    def at_h(place):
        return (place * NX + x, tp)

    def at_tp(zz, ll, cc):
        return (dp, zz * 4 + ll * 2 + cc)

    def z_at(offset):
        return lax.rem(z + (offset + NZ), NZ)

    def slot(offset):
        return (offset + NZ) % NZ

    across_l, across_c = at_tp(z, other_l, c), at_tp(z, l, other_c)
    sent = []

    def send(src, dst, send_sem, recv_sem, device, listed_copy=True):
        copy = pltpu.make_async_remote_copy(
            src_ref=src, dst_ref=dst, send_sem=send_sem, recv_sem=recv_sem,
            device_id=device, device_id_type=pl.DeviceIdType.MESH,
        )
        copy.start()
        if listed_copy:
            sent.append(copy)

    def arrived(dst, send_sem, recv_sem, device):
        pltpu.make_async_remote_copy(
            src_ref=dst, dst_ref=dst, send_sem=send_sem, recv_sem=recv_sem,
            device_id=device, device_id_type=pl.DeviceIdType.MESH,
        ).wait_recv()

    loads = [
        pltpu.make_async_copy(src, dst, load_sem.at[i])
        for i, (src, dst) in enumerate(
            ((pool.at[:, pl.ds(0, KVH * HD)], pool_v.at[:, pl.ds(0, KVH * HD)]), (pool.at[:, pl.ds(KVH * HD, KVH * HD)], pool_v.at[:, pl.ds(KVH * HD, KVH * HD)]), (gate_w, gate_v), (up_w, up_v), (down_w, down_v))
        )
    ]
    for copy in loads[:2]:
        copy.start()
    waiting = set(range(len(loads)))

    def use(i):
        if i in waiting:
            waiting.discard(i)
            loads[i].wait()


    others = [lax.rem(h + o // NX, NH) * NX + lax.rem(x + o % NX, NX) for o in DISTANCES]
    barrier = pltpu.get_barrier_semaphore()
    partners = [at_dp(rank) for rank in others]
    partners += [at_tp(z_at(o), l, c) for o in range(1, NZ)] + [across_l, across_c]
    for device in partners:
        pl.semaphore_signal(barrier, inc=1, device_id=device, device_id_type=pl.DeviceIdType.MESH)

    def exchange(src, dst, s_sem, r_sem):
        for rank in others:
            send(src.at[rank], dst.at[dp], s_sem, r_sem, at_dp(rank), False)
        dst[dp] = src[dp]

    def exchanged(dst, s_sem, r_sem):
        arrived(dst.at[pl.ds(0, DP - 1)], s_sem, r_sem, at_dp(others[0]))

    def all_left(src, s_sem, r_sem):
        part = src.at[pl.ds(0, DP - 1)]
        pltpu.make_async_remote_copy(
            src_ref=part, dst_ref=part, send_sem=s_sem, recv_sem=r_sem,
            device_id=at_dp(others[0]), device_id_type=pl.DeviceIdType.MESH,
        ).wait_send()

    slot_id = mig[0, 0, 0]
    second = slot_id == 1

    def ordered(value):
        return jnp.where(second, value, jnp.concatenate([value[1:2], value[0:1]], axis=0))

    for source, dst, count in ((q_in, q_t, 64), (res_in, res_t, 64), (new_in, new_t, 16)):
        value = ordered(source[...].astype(F32))
        for j in range(count):
            dst[pl.ds(j, 2, stride=count), :] = value[:, j * HD : (j + 1) * HD]

    top_half = lax.broadcasted_iota(jnp.int32, (KVH, 8, HD), 1) < 4

    def turned(value):
        return jnp.concatenate([value[:, 4:], value[:, :4]], axis=1)

    def pieces(first, second_value):
        even = jnp.where(top_half, first, turned(second_value))
        odd = jnp.where(top_half, turned(first), second_value)
        return even, odd


    def bias_of(place):
        lane = lax.broadcasted_iota(jnp.int32, (8, MAXP * 2 * PG), 1)
        page, inner = lane >> 4, lane & 15
        length = lengths[place]
        filled = jnp.zeros_like(lane)
        for p in range(MAXP):
            held = jnp.minimum(jnp.maximum(length - p * PG, 0), PG)
            filled = jnp.where(page == table[place, p], held, filled)
        return jnp.where(inner < filled, 0.0, -1e30)

    def attend(q_rows, new_rows, hidden_bias, first):
        count = q_rows.shape[0]
        heads = range(first, first + count)
        factor = 1.0 / math.sqrt(HD)
        new_keys = jnp.stack([new_rows[j : j + 1] for j in heads])
        new_values = jnp.stack([new_rows[KVH + j : KVH + j + 1] for j in heads])
        q_bf = q_rows.astype(BF)
        score = jnp.stack(
            [
                lax.dot_general(
                    q_bf[j - first], pool_v[:, j * HD : (j + 1) * HD],
                    (((1,), (1,)), ((), ())), preferred_element_type=F32,
                )
                for j in heads
            ]
        )
        score = score * factor + hidden_bias[None]
        own_score = jnp.sum(q_rows * new_keys, axis=-1, keepdims=True) * factor
        top = jnp.maximum(jnp.max(score, axis=-1, keepdims=True), own_score)
        exponent = jnp.exp(score - top)
        own_exponent = jnp.exp(own_score - top)
        scale = 1.0 / (jnp.sum(exponent, axis=-1, keepdims=True) + own_exponent)
        weight = (exponent * scale).astype(BF)
        own_weight = (own_exponent * scale).astype(BF).astype(F32)
        use(1)
        attended = jnp.stack(
            [
                jnp.dot(
                    weight[j - first], pool_v[:, (KVH + j) * HD : (KVH + j + 1) * HD],
                    preferred_element_type=F32,
                )
                for j in heads
            ]
        )
        return attended + own_weight * new_values

    def normalise(res_rows, attended):
        stream = res_rows + attended
        square = jnp.sum(jnp.sum(stream * stream, axis=0), axis=-1, keepdims=True)
        mean = jnp.sum(square, axis=0, keepdims=True) * (1.0 / (DP * 4 * HD))
        scale = lax.rsqrt(mean + EPSILON)
        return stream * scale[None] * gain[...].astype(F32).reshape(KVH, 8, HD), stream

    lines = (line_q, line_res)

    def local(_):
        local_q = q_t[:64].reshape(KVH, 8, HD)
        local_res = res_t[:64].reshape(KVH, 8, HD)
        hidden_bias = bias_of(1 - slot_id)
        use(0)
        for copy in loads[2:]:
            copy.start()
        normed, stream = normalise(local_res, attend(local_q, new_t[:16], hidden_bias, 0))
        stream_local[...] = stream.reshape(DP * 4, HD)
        for k in range(DP):
            c_local[k] = normed[k // 2, 4 * (k % 2) : 4 * (k % 2) + 4]
        pl.semaphore_wait(barrier, len(partners))
        exchange(c_local, in_local, c_s.at[0], c_r.at[0])
        own[...] = jnp.concatenate([q_t[64:], new_t[16:], res_t[64:]], axis=0).astype(BF)
        for i, rows in enumerate(ROUTED):
            for o in range(1, NX):
                place = lax.rem(x + o, NX)
                send(
                    own.at[rows], lines[i].at[x], rx_s.at[i, o - 1], rx_r.at[i, o - 1],
                    (h * NX + place, tp),
                )
            lines[i][x] = own[rows]

    sources = [mig[i, 0, 1] for i in range(MIG)]
    targets = [mig[i, 0, 2] for i in range(MIG)]

    def route(i):
        span_of = ROUTED[i]
        for o in range(1, NX):
            place = lax.rem(x + NX - o, NX)
            arrived(
                lines[i].at[place], rx_s.at[i, o - 1], rx_r.at[i, o - 1],
                (h * NX + place, tp),
            )
        rows = [lines[i][lax.rem(target, NX)].astype(F32) for target in targets]
        here = [lax.div(target, NX) == h for target in targets]

        def wanted(rank):
            value = jnp.zeros_like(rows[0])
            for j in range(MIG):
                value = jnp.where(here[j] & (sources[j] == rank), rows[j], value)
            return value.astype(BF)

        for o in range(1, NH):
            place = lax.rem(h + o, NH)
            y_send[o - 1, span_of] = wanted(place * NX + x)
            send(
                y_send.at[o - 1, span_of], y_recv.at[o - 1, span_of],
                ry_s.at[i, o - 1], ry_r.at[i, o - 1], at_h(place),
            )
        y_recv[NH - 1, span_of] = wanted(dp)

    def routed(i):
        span_of = ROUTED[i]
        for o in range(1, NH):
            arrived(
                y_recv.at[o - 1, span_of], ry_s.at[i, o - 1], ry_r.at[i, o - 1],
                at_h(lax.rem(h + NH - o, NH)),
            )
        row = y_recv[NH - 1, span_of].astype(F32)
        for o in range(NH - 1):
            row = row + y_recv[o, span_of].astype(F32)
        serves = (sources[0] == dp) | (sources[1] == dp) | (sources[2] == dp)
        return jnp.where(serves, row, own[span_of].astype(F32))

    def listed(part):
        if part == 0:
            routed_row[...] = routed(0)
            bias_row[...] = bias_of(slot_id)
        if part < 2:
            q_rows = routed_row[32 * part : 32 * part + 32].reshape(4, 8, HD)
            attended_row[4 * part : 4 * part + 4] = attend(
                q_rows, routed_row[64:], bias_row[...], 4 * part
            )
        else:
            normed, stream = normalise(routed(1).reshape(KVH, 8, HD), attended_row[...])
            even, odd = pieces(normed, stream)
            for k in range(DP):
                c_listed[k] = (even, odd)[k % 2][k // 2]
            exchange(c_listed, in_listed, c_s.at[1], c_r.at[1])

    def start_x(w):
        source, count = (in_local, 4) if w == 0 else (in_listed, 8)
        exchanged(source, c_s.at[w], c_r.at[w])
        for a in range(DP):
            tiles[count * a : count * a + count] = source[a]
        x_all[w, z, c, l] = jnp.concatenate(
            [tiles[pl.ds(i, DP, stride=count), :] for i in range(4)], axis=1
        ).astype(BF)
        block = x_all.at[w, z, c, l]
        send(block, block, xl_s.at[w], xl_r.at[w], across_l)

    def start_y(w):
        arrived(x_all.at[w, z, c, other_l], xl_s.at[w], xl_r.at[w], across_l)
        block = x_all.at[w, z, c]
        send(block, block, xc_s.at[w, 0], xc_r.at[w, 0], across_c)
        offsets = [o for kind, places in CHUNKS if kind == w for o in places if o]
        for o in offsets:
            send(block, block, xz_s.at[w, slot(o)], xz_r.at[w, slot(o)], at_tp(z_at(-o), l, c))

    def forward(q):
        w, offsets = CHUNKS[q]
        for o in offsets:
            if o:
                zz = z_at(o)
                block = x_all.at[w, zz, c]
                arrived(block, xz_s.at[w, slot(o)], xz_r.at[w, slot(o)], at_tp(zz, l, c))
                send(block, block, xc_s.at[w, slot(o)], xc_r.at[w, slot(o)], across_c)

    def span(q):
        return pl.ds(STARTS[q], SIZES[q])

    def stage_a(q):
        w, offsets = CHUNKS[q]
        for o in offsets:
            arrived(x_all.at[w, z_at(o), other_c], xc_s.at[w, slot(o)], xc_r.at[w, slot(o)], across_c)
        use(2)
        use(3)
        rows = jnp.concatenate([x_all[w, z_at(o)].reshape(64, 512) for o in offsets], axis=0)
        part_rows = span(q)
        for weight, dst in ((gate_v, gate_p), (up_v, up_p)):
            value = jnp.dot(rows, weight[...], preferred_element_type=F32).astype(BF)
            dst[:, part_rows] = value.reshape(NX, SIZES[q], 512)
        send(gate_p.at[xo, part_rows], m1g.at[part_rows], xp_s.at[q, 0], xp_r.at[q, 0], right)
        send(up_p.at[xo, part_rows], m1u.at[part_rows], xp_s.at[q, 1], xp_r.at[q, 1], left)
        send(up_p.at[xr, part_rows], m2u.at[part_rows], xp_s.at[q, 2], xp_r.at[q, 2], right)
        send(gate_p.at[xl, part_rows], m2g.at[part_rows], xp_s.at[q, 3], xp_r.at[q, 3], left)

    def stage_b(q):
        t = span(q)
        arrived(m1g.at[t], xp_s.at[q, 0], xp_r.at[q, 0], left)
        s3g[t] = (gate_p[xr, t].astype(F32) + m1g[t].astype(F32)).astype(BF)
        send(s3g.at[t], m3g.at[t], xp_s.at[q, 4], xp_r.at[q, 4], right)
        arrived(m1u.at[t], xp_s.at[q, 1], xp_r.at[q, 1], right)
        s3u[t] = (up_p[xl, t].astype(F32) + m1u[t].astype(F32)).astype(BF)
        send(s3u.at[t], m3u.at[t], xp_s.at[q, 5], xp_r.at[q, 5], left)

    def stage_c(q):
        t = span(q)
        arrived(m2u.at[t], xp_s.at[q, 2], xp_r.at[q, 2], left)
        arrived(m2g.at[t], xp_s.at[q, 3], xp_r.at[q, 3], right)
        arrived(m3g.at[t], xp_s.at[q, 4], xp_r.at[q, 4], left)
        arrived(m3u.at[t], xp_s.at[q, 5], xp_r.at[q, 5], right)
        gate = gate_p[x, t].astype(F32) + m2g[t].astype(F32) + m3g[t].astype(F32)
        up = up_p[x, t].astype(F32) + m2u[t].astype(F32) + m3u[t].astype(F32)
        gate, up = gate.astype(BF), up.astype(BF)
        for b in range(NH):
            columns = slice(b * HD, (b + 1) * HD)
            h_send[b, t] = jnp.concatenate([gate[:, columns], up[:, columns]], axis=1)
        for o in (2, 1, 3):
            place = lax.rem(h + o, NH)
            send(
                h_send.at[place, t], h_recv.at[o - 1, t],
                hp_s.at[q, o - 1], hp_r.at[q, o - 1], at_h(place),
            )

    def stage_d(q):
        t = span(q)
        for o in range(1, NH):
            arrived(
                h_recv.at[o - 1, t], hp_s.at[q, o - 1], hp_r.at[q, o - 1],
                at_h(lax.rem(h + NH - o, NH)),
            )
        total = h_send[h, t].astype(F32)
        for o in range(NH - 1):
            total = total + h_recv[o, t].astype(F32)
        gate, up = total[:, :HD], total[:, HD:]
        hid[x, h, t] = (gate / (1.0 + jnp.exp(-gate)) * up).astype(BF)
        block = hid.at[x, h, t]
        for o in (2, 1, 3):
            send(
                block, block, hg_s.at[q, o - 1], hg_r.at[q, o - 1], at_h(lax.rem(h + o, NH))
            )

    def stage_e(q):
        t = span(q)
        for o in range(1, NH):
            place = lax.rem(h + NH - o, NH)
            arrived(hid.at[x, place, t], hg_s.at[q, o - 1], hg_r.at[q, o - 1], at_h(place))
        block = hid.at[x, pl.ds(0, NH), t]
        send(block, block, xg_s.at[q, 0], xg_r.at[q, 0], right)
        send(block, block, xg_s.at[q, 1], xg_r.at[q, 1], left)

    def stage_f(q):
        t = span(q)
        arrived(hid.at[xl, pl.ds(0, NH), t], xg_s.at[q, 0], xg_r.at[q, 0], left)
        half = hid.at[xl, pl.ds(0, 2), t]
        send(half, half, xg_s.at[q, 2], xg_r.at[q, 2], right)
        arrived(hid.at[xr, pl.ds(0, NH), t], xg_s.at[q, 1], xg_r.at[q, 1], right)
        half = hid.at[xr, pl.ds(2, 2), t]
        send(half, half, xg_s.at[q, 3], xg_r.at[q, 3], left)

    def stage_g(q):
        t = span(q)
        arrived(hid.at[xo, pl.ds(0, 2), t], xg_s.at[q, 2], xg_r.at[q, 2], left)
        arrived(hid.at[xo, pl.ds(2, 2), t], xg_s.at[q, 3], xg_r.at[q, 3], right)
        use(4)
        rows = jnp.concatenate(
            [jnp.concatenate([hid[a, b, t] for b in range(NH)], axis=1) for a in range(NX)], axis=0
        )
        value = jnp.dot(rows, down_v[...], preferred_element_type=F32).astype(BF)
        count, first_block = SIZES[q] // 16, STARTS[q] // 16
        value = value.reshape(count, 2, 2, 16, 512)
        for b in range(count):
            part[:, first_block + b] = value[b]
        blocks = pl.ds(first_block, count)
        send(part.at[other_c, blocks], part_in.at[blocks], oc_s.at[q], oc_r.at[q], across_c)

    def stage_h(q):
        w, offsets = CHUNKS[q]
        first_block = STARTS[q] // 16
        blocks = pl.ds(first_block, SIZES[q] // 16)
        arrived(part_in.at[blocks], oc_s.at[q], oc_r.at[q], across_c)
        z_send[blocks] = (part[c, blocks].astype(F32) + part_in[blocks].astype(F32)).astype(BF)
        for b, o in enumerate(offsets):
            if o:
                send(
                    z_send.at[first_block + b], z_recv.at[w, slot(o)],
                    oz_s.at[w, slot(o)], oz_r.at[w, slot(o)], at_tp(z_at(o), l, c),
                )

    def start_l(w):
        offsets = []
        for q, (kind, places) in enumerate(CHUNKS):
            for b, o in enumerate(places):
                if kind == w and o:
                    offsets.append(o)
                elif kind == w:
                    total = z_send[STARTS[q] // 16 + b].astype(F32)
        for o in offsets:
            arrived(
                z_recv.at[w, slot(o)], oz_s.at[w, slot(o)], oz_r.at[w, slot(o)],
                at_tp(z_at(-o), l, c),
            )
            total = total + z_recv[w, slot(o)].astype(F32)
        l_send[w] = total.astype(BF)
        send(l_send.at[w, other_l], l_recv.at[w], ol_s.at[w], ol_r.at[w], across_l)

    def start_m(w):
        arrived(l_recv.at[w], ol_s.at[w], ol_r.at[w], across_l)
        ffn = l_send[w, l].astype(F32) + l_recv[w].astype(F32)
        for i in range(4):
            rows_out[w, pl.ds(i, DP, stride=4), :] = ffn[:, i * HD : (i + 1) * HD]
        if w == 0:
            for rank in range(DP):
                e_send[0, rank] = rows_out[0, 4 * rank : 4 * rank + 4]
        else:
            for rank in range(DP):
                fin[rank] = rows_out[1, 4 * rank : 4 * rank + 4] + in_listed[rank, 4:]
            for rank in range(DP):
                anchor = jnp.int32(rank)
                for i in range(MIG):
                    anchor = jnp.where(targets[i] == rank, sources[i], anchor)
                e_send[1, rank] = fin[anchor]
        exchange(e_send.at[w], e_recv.at[w], e_s.at[w], e_r.at[w])

    steps = {
        "local": local, "route": route, "listed": listed, "x": start_x, "y": start_y,
        "w": forward, "a": stage_a, "b": stage_b, "c": stage_c, "d": stage_d, "e": stage_e,
        "f": stage_f, "g": stage_g, "h": stage_h, "l": start_l, "m": start_m,
    }
    counts, left_behind = [], 0
    for step in ORDER:
        name = step.rstrip("0123456789")
        steps[name](int(step[len(name) :] or 0))
        counts.append(len(sent))
        if len(counts) > LAG:
            while left_behind < counts[-LAG]:
                sent[left_behind].wait_send()
                left_behind += 1

    all_left(c_local, c_s.at[0], c_r.at[0])
    all_left(c_listed, c_s.at[1], c_r.at[1])
    for copy in sent[left_behind:]:
        copy.wait_send()
    for w in range(2):
        exchanged(e_recv.at[w], e_s.at[w], e_r.at[w])
        for k in range(DP):
            tiles[64 * w + 4 * k : 64 * w + 4 * k + 4] = e_recv[w, k]
    tiles[:64] = tiles[:64] + stream_local[...]
    stays, moved = tiles[:64], tiles[64:]
    out[:64] = jnp.where(second, stays, moved).astype(BF)
    out[64:] = jnp.where(second, moved, stays).astype(BF)
    for w in range(2):
        all_left(e_send.at[w], e_s.at[w], e_r.at[w])


def on_device(
    queries, residual, new_entries, page_pool, page_table, cache_lengths, migration,
    norm_gain, gate_weight, up_weight, down_weight,
):
    pages, page_rows, entry = page_pool.shape[2:]
    vmem = pl.BlockSpec(memory_space=pltpu.VMEM)
    hbm = pl.BlockSpec(memory_space=pl.ANY)
    smem = pl.BlockSpec(memory_space=pltpu.SMEM)
    nq = len(CHUNKS)
    dma = pltpu.SemaphoreType.DMA
    share = (256, 512)
    scratch = [
        pltpu.VMEM((512, 2048), BF),
        pltpu.VMEM((512, 512), BF), pltpu.VMEM((512, 512), BF), pltpu.VMEM((512, 512), BF),
        pltpu.VMEM((128, HD), F32), pltpu.VMEM((128, HD), F32), pltpu.VMEM((32, HD), F32),
        pltpu.VMEM((144, HD), BF), pltpu.VMEM((NX, 80, HD), BF), pltpu.VMEM((NX, 64, HD), BF),
        pltpu.VMEM((NH - 1, 144, HD), BF), pltpu.VMEM((NH, 144, HD), BF),
        pltpu.VMEM((DP, 4, HD), F32), pltpu.VMEM((DP, 8, HD), F32),
        pltpu.VMEM((DP, 4, HD), F32), pltpu.VMEM((DP, 8, HD), F32),
        pltpu.VMEM((64, HD), F32), pltpu.VMEM((80, HD), F32), pltpu.VMEM((KVH, 8, HD), F32),
        pltpu.VMEM((8, MAXP * 2 * PG), F32), pltpu.VMEM((DP * 8, HD), F32),
        pltpu.VMEM((2, NZ, 2, 2, 16, 512), BF),
        pltpu.VMEM((NX,) + share, BF), pltpu.VMEM((NX,) + share, BF),
    ]
    scratch += [pltpu.VMEM(share, BF) for _ in range(8)]
    scratch += [
        pltpu.VMEM((NH, 256, 256), BF), pltpu.VMEM((NH - 1, 256, 256), BF),
        pltpu.VMEM((NX, NH, 256, HD), BF),
        pltpu.VMEM((2, 16, 2, 16, 512), BF), pltpu.VMEM((16, 2, 16, 512), BF),
        pltpu.VMEM((16, 2, 16, 512), BF), pltpu.VMEM((2, NZ, 2, 16, 512), BF),
        pltpu.VMEM((2, 2, 16, 512), BF), pltpu.VMEM((2, 16, 512), BF),
        pltpu.VMEM((2, 64, HD), F32), pltpu.VMEM((DP, 4, HD), F32),
        pltpu.VMEM((2, DP, 4, HD), F32), pltpu.VMEM((2, DP, 4, HD), F32),
    ]
    scratch += [dma((5,))]
    scratch += [dma((2, 3)) for _ in range(4)]
    scratch += [dma((2,)), dma((2,)), dma((2,)), dma((2,))]
    scratch += [dma((2,)), dma((2,)), dma((2, NZ)), dma((2, NZ)), dma((2, NZ)), dma((2, NZ))]
    scratch += [dma((nq, 6)), dma((nq, 6)), dma((nq, 3)), dma((nq, 3)), dma((nq, 3)), dma((nq, 3))]
    scratch += [dma((nq, 4)), dma((nq, 4)), dma((nq,)), dma((nq,)), dma((2, NZ)), dma((2, NZ))]
    scratch += [dma((2,)), dma((2,))]
    done = pl.pallas_call(
        kernel,
        out_shape=jax.ShapeDtypeStruct((2 * DP * 4, HD), BF),
        in_specs=[smem, smem, smem, vmem, vmem, vmem, vmem, hbm, hbm, hbm, hbm],
        out_specs=vmem,
        scratch_shapes=scratch,
        compiler_params=pltpu.CompilerParams(
            collective_id=0, has_side_effects=True, vmem_limit_bytes=62 * 1024 * 1024
        ),
    )(
        migration.transpose(1, 0, 2), page_table[0, 0], cache_lengths[0, 0],
        queries[0, 0], residual[0, 0], new_entries[0, 0], norm_gain.reshape(DP * 4, HD),
        page_pool.reshape(pages * page_rows, entry), gate_weight, up_weight, down_weight,
    )
    return done.reshape(1, 1, 2, DP * 4 * HD)


def solution(mesh):
    return jax.shard_map(
        on_device,
        mesh=mesh,
        in_specs=(
            P("dp", "tp", None, None),
            P("dp", "tp", None, None),
            P("dp", "tp", None, None),
            P("dp", "tp", None, None, None),
            P("dp", "tp", None, None),
            P("dp", "tp", None),
            P("tp", None, None),
            P(),
            P("dp", "tp"),
            P("dp", "tp"),
            P("tp", "dp"),
        ),
        out_specs=P("dp", "tp", None, None),
        check_vma=False,
    )
```
